32 devices in a mesh: parts: 2 (over y), blk: 16 (over z, x, core).
Axes of the slice: x: 2, y: 2, z: 4, core: 2. Of those that a mesh axis runs over, the one named last changes fastest.
Arguments:
- embedding: float32 [16384, 768], P(('parts', 'blk')), parts along dimension 0
- row_owner: int32 [16384], P(('parts', 'blk')), parts along dimension 0, may hold values from 0 to 15, as said below
- cluster_id: int32 [16384], P(('parts', 'blk')), parts along dimension 0, may hold values from 0 to 63, as said below
Outputs:
- nearest: float32 [16384], P(('parts', 'blk')), parts along dimension 0
The draws below stay inside these ranges and needn't reach their ends.
There are 2 independent parts, one for each index of `parts`. The reference program is written for one: setup_inputs(seed, part) draws one part's arguments, and reference() takes and returns one part's arrays. A program takes and returns all parts, laid end to end along the dimension named above; each array names one. Nothing has to cross between parts.
Inputs may be any that keep to these rules, and one draw needn't show every extreme that they name: Among the 512 rows of one blk device at most 64 have the same owner, and some owner gets exactly 64; row_owner // 4 equals cluster_id // 16. cluster_id // 16 is the owner group of the cluster.
All inputs are finite; a program needn't handle non-finite values.
Results may differ from the reference program's by a relative error of at most 0.0003.
Values may be sent and summed in bfloat16 or wider, within the bound.
No kernel may reach another device: no remote copies, remote signals or barrier semaphores. Data moves between devices by JAX's collectives and lax.ppermute only.
A program may use at most 64 MiB of HBM per device.

```python
import math
import jax
import jax.numpy as jnp
from jax import lax

D = 768
ROWS_DEV = 512
GROUP = 4
CPG = 16
CAP = 64
ROWS = 8192
CLUSTERS = 64
N_BLK = 16


def routing(key):
    slots = N_BLK * CAP
    extra_random_key, block_random_key = jax.random.split(key)
    extra_credit = jax.random.randint(extra_random_key, (N_BLK,), 0, 4) * 1024
    slot_holder = jnp.arange(slots, dtype=jnp.int32) // CAP

    def one_block(bkey):
        kf, kb, kp, kc, kt = jax.random.split(bkey, 5)
        filled_slots = jax.random.randint(kf, (), 0, N_BLK)
        base_offset = jax.random.randint(kb, (slots,), 0, 1024)
        match_score = base_offset + extra_credit[slot_holder] + jnp.where(slot_holder == filled_slots, 8192, 0)
        match_score = match_score * slots + jnp.arange(slots, dtype=jnp.int32)
        chosen = jnp.argsort(-match_score)[:ROWS_DEV]
        owners = (chosen // CAP)[jax.random.permutation(kp, ROWS_DEV)]
        upper = jax.random.randint(kt, (ROWS_DEV,), 1, CPG + 1)
        local = jax.random.randint(kc, (ROWS_DEV,), 0, upper)
        return (owners.astype(jnp.int32), (owners // GROUP * CPG + local).astype(jnp.int32))
    owners, clusters = jax.vmap(one_block)(jax.random.split(block_random_key, N_BLK))
    return (owners.reshape(-1), clusters.reshape(-1))


def draw_row_owner(key, part):
    return routing(key)[0]


def draw_cluster_id(key, part):
    return routing(key)[1]


def draw_embedding(key, part):
    owners, clusters = routing(key)
    key = jax.random.fold_in(key, 11)
    kc = jax.random.fold_in(key, 0)
    kn = jax.random.fold_in(key, 1)
    kb = jax.random.fold_in(key, 2)
    kg = jax.random.fold_in(key, 4)
    kp = jax.random.fold_in(key, 5)
    kd = jax.random.fold_in(key, 6)
    km = jax.random.fold_in(key, 7)
    group_count = CLUSTERS // CPG
    shared = jax.random.normal(kg, (group_count, D), jnp.float32)
    centers = shared[jnp.arange(CLUSTERS, dtype=jnp.int32) // CPG] + 0.2 * jax.random.normal(kc, (CLUSTERS, D), jnp.float32)
    spread = jnp.exp(jax.random.uniform(kb, (ROWS, 1), jnp.float32, math.log(0.1), math.log(4.0)))
    shuffle = jax.random.permutation(kp, ROWS).astype(jnp.int32)
    order = jnp.argsort(clusters * ROWS + shuffle).astype(jnp.int32)
    sorted_cluster = clusters[order]
    previous = jnp.roll(order, 1)
    position = jnp.arange(ROWS, dtype=jnp.int32)
    coin = jax.random.randint(kd, (ROWS,), 0, 5) < 3
    paired = (position % 2 == 1) & (sorted_cluster == jnp.roll(sorted_cluster, 1)) & coin
    source = jnp.zeros((ROWS,), jnp.int32).at[order].set(jnp.where(paired, previous, order))
    copied = jnp.zeros((ROWS, 1), jnp.float32).at[order].set(jnp.where(paired, 1.0, 0.0).astype(jnp.float32)[:, None])
    noise = jax.random.normal(kn, (ROWS, D), jnp.float32)
    extra = jax.random.normal(km, (ROWS, D), jnp.float32)
    return centers[clusters] + spread[source] * (noise[source] + 0.1 * copied * extra)


def setup_inputs(seed: int = 0, part: int = 0) -> dict:
    key_of = jax.random.split(jax.random.key(seed), 4)
    part_splits = jax.random.split(jax.random.fold_in(key_of[3], part), 4)
    return {
        "embedding": draw_embedding(jax.random.fold_in(jax.random.fold_in(key_of[3], part), 71), part),
        "row_owner": draw_row_owner(jax.random.fold_in(jax.random.fold_in(key_of[3], part), 71), part),
        "cluster_id": draw_cluster_id(jax.random.fold_in(jax.random.fold_in(key_of[3], part), 71), part),
    }


def reference(embedding, row_owner, cluster_id):
    squares = lax.optimization_barrier(jnp.sum(embedding * embedding, axis=1, keepdims=True))
    unit = (embedding * lax.rsqrt(squares + 1e-06)).astype(jnp.bfloat16).astype(jnp.float32)
    width = unit.shape[1]
    window = GROUP * N_BLK * CAP
    block = 256
    order = jnp.argsort(row_owner // GROUP, stable=True).astype(jnp.int32)
    padded = jnp.concatenate([jnp.zeros((window, width), jnp.float32), unit[order], jnp.zeros((window, width), jnp.float32)], axis=0)
    labels = jnp.concatenate([jnp.full((window,), -2, jnp.int32), cluster_id[order], jnp.full((window,), -2, jnp.int32)])
    indices = jnp.concatenate([jnp.full((window,), -1, jnp.int32), order, jnp.full((window,), -1, jnp.int32)])

    def one_block(number):
        start = (number * block).astype(jnp.int32)
        query = lax.dynamic_slice_in_dim(padded, start + window, block, 0)
        q_label = lax.dynamic_slice_in_dim(labels, start + window, block, 0)
        q_index = lax.dynamic_slice_in_dim(indices, start + window, block, 0)
        keys = lax.dynamic_slice_in_dim(padded, start, 2 * window + block, 0)
        k_label = lax.dynamic_slice_in_dim(labels, start, 2 * window + block, 0)
        k_index = lax.dynamic_slice_in_dim(indices, start, 2 * window + block, 0)
        scores = jnp.dot(query, keys.T, preferred_element_type=jnp.float32, precision=lax.Precision.HIGHEST)
        allowed = (q_label[:, None] == k_label[None, :]) & (q_index[:, None] != k_index[None, :])
        return lax.optimization_barrier(jnp.max(jnp.where(allowed, scores, jnp.float32(-1.0)), axis=1))
    sorted_best = lax.map(one_block, jnp.arange(ROWS // block, dtype=jnp.int32)).reshape(-1)
    return jnp.zeros((ROWS,), jnp.float32).at[order].set(sorted_best)
```

```python
import jax
import jax.numpy as jnp
from jax import lax
from jax.experimental import pallas as pl
from jax.experimental.pallas import tpu as pltpu
from jax.sharding import PartitionSpec as P

GROUP = 4
STAGES = 4
NT = (((1,), (1,)), ((), ()))


def iota(shape, axis):
    return lax.broadcasted_iota(jnp.int32, shape, axis)


def pack_kernel(groups, cap, emb_ref, owner_ref, cluster_ref, *outs):
    blocks, label_ref, slot_ref = outs[:STAGES], outs[STAGES], outs[STAGES + 1]
    rows = emb_ref.shape[0]
    x = emb_ref[...]
    squares = jnp.sum(x * x, axis=1, keepdims=True)
    unit = (x * lax.rsqrt(squares + 1e-06)).astype(jnp.bfloat16)
    mine = lax.axis_index("blk") // GROUP
    rel = (owner_ref[...] >> 2) ^ mine
    tall = max(groups, 16)
    member = iota((tall, rows), 0) == rel
    earlier = (iota((rows, rows), 0) < iota((rows, rows), 1)).astype(jnp.bfloat16)
    count = jnp.dot(member.astype(jnp.bfloat16), earlier, preferred_element_type=jnp.float32)
    rank = jnp.sum(jnp.where(member, count, 0.0), axis=0, keepdims=True)
    slot = rel * cap + rank.astype(jnp.int32)
    slot_ref[...] = slot
    label = ((cluster_ref[...] & 15) + 1).astype(jnp.float32).astype(jnp.bfloat16)
    label = jnp.broadcast_to(label, (16, rows))
    size = groups * cap // STAGES
    for s in range(STAGES):
        hot = (iota((size, rows), 0) + s * size == slot).astype(jnp.bfloat16)
        blocks[s][...] = jnp.dot(hot, unit, preferred_element_type=jnp.float32).astype(jnp.bfloat16)
        packed = lax.dot_general(label, hot, NT, preferred_element_type=jnp.float32)
        label_ref[:, s * size : (s + 1) * size] = packed[0:1, :] - 1.0


def pack(groups, cap, embedding, owner, cluster):
    rows, width = embedding.shape
    size = groups * cap // STAGES
    block = jax.ShapeDtypeStruct((size, width), jnp.bfloat16)
    return pl.pallas_call(
        lambda *refs: pack_kernel(groups, cap, *refs),
        out_shape=[block] * STAGES
        + [
            jax.ShapeDtypeStruct((1, groups * cap), jnp.float32),
            jax.ShapeDtypeStruct((1, rows), jnp.int32),
        ],
        compiler_params=pltpu.CompilerParams(vmem_limit_bytes=48 << 20),
        name="pack",
    )(embedding, owner.reshape(1, rows), cluster.reshape(1, rows))


def compare_kernel(stage, labels_ref, *refs):
    keys, best_ref, out_ref = refs[: 4 * stage + 4], refs[4 * stage + 4], refs[-1]
    size = keys[0].shape[0]

    def tile(q, k, peer, best):
        scores = lax.dot_general(
            keys[4 * k + peer][...], keys[4 * q][...], NT, preferred_element_type=jnp.float32
        )
        mine = labels_ref[0:1, q * size : (q + 1) * size]
        allowed = columns[k][:, peer : peer + 1] == mine
        if peer == 0 and q == k:
            allowed = allowed & (iota((size, size), 0) != iota((size, size), 1))
        return jnp.maximum(best, jnp.max(jnp.where(allowed, scores, -1.0), axis=0, keepdims=True))

    columns = [labels_ref[:, k * size : (k + 1) * size].T for k in range(stage + 1)]
    for q in range(stage + 1):
        if q < stage:
            best = best_ref[:, q * size : (q + 1) * size]
        else:
            best = jnp.full((1, size), -1.0, jnp.float32)
        for k in range(stage + 1) if q == stage else [stage]:
            for peer in range(4):
                best = tile(q, k, peer, best)
        out_ref[:, q * size : (q + 1) * size] = best


def compare(stage, labels, keys, best):
    size, width = keys[0].shape
    tiles = 8 * stage + 4
    return pl.pallas_call(
        lambda *refs: compare_kernel(stage, *refs),
        out_shape=jax.ShapeDtypeStruct((1, (stage + 1) * size), jnp.float32),
        compiler_params=pltpu.CompilerParams(vmem_limit_bytes=48 << 20),
        cost_estimate=pl.CostEstimate(
            flops=2 * tiles * size * size * width,
            bytes_accessed=len(keys) * size * width * 2,
            transcendentals=0,
        ),
        name=f"compare{stage}",
    )(labels, *keys, best)


def unpack_kernel(slot_ref, *refs):
    out_ref = refs[-1]
    slot = slot_ref[...]
    rows = slot.shape[1]
    total = jnp.zeros((8, rows), jnp.float32)
    start = 0
    for ref in refs[:-1]:
        size = ref.shape[1]
        column = jnp.broadcast_to(ref[...], (8, size)).T[:, 0:1]
        hit = iota((size, rows), 0) + start == slot
        part = jnp.where(hit, column, 0.0)
        total = total + jnp.sum(part.reshape(size // 8, 8, rows), axis=0)
        start += size
    out_ref[...] = jnp.sum(total, axis=0, keepdims=True)


def unpack(slot, backs):
    return pl.pallas_call(
        unpack_kernel,
        out_shape=jax.ShapeDtypeStruct(slot.shape, jnp.float32),
        name="unpack",
    )(slot, *backs)


def on_device(embedding, row_owner, cluster_id):
    rows, _ = embedding.shape
    devices = lax.axis_size("blk")
    groups = devices // GROUP
    cap = GROUP * max(2, 2 * rows // devices)
    size = groups * cap // STAGES
    per_stage = groups // STAGES

    def swap(array, mask):
        return lax.ppermute(array, "blk", [(i, i ^ mask) for i in range(devices)])

    sends = pack(groups, cap, embedding, row_owner, cluster_id)
    blocks, label, slot = sends[:STAGES], sends[STAGES], sends[STAGES + 1]
    every = lax.all_gather(label.reshape(groups * cap), "blk").reshape(devices, groups, cap)
    mine = lax.axis_index("blk")
    steps = jnp.arange(groups)
    sources = (mine ^ jnp.arange(4)[:, None]) ^ (steps[None, :] * GROUP)
    labels = every[sources, steps[None, :]].reshape(4, groups * cap)
    labels = jnp.concatenate([labels, labels], axis=0)

    keys, best = [], jnp.full((1, 128), -1.0, jnp.float32)
    for s in range(STAGES):
        pieces = []
        for d in range(s * per_stage, (s + 1) * per_stage):
            piece = blocks[s][(d - s * per_stage) * cap : (d - s * per_stage + 1) * cap]
            pieces.append(swap(piece, d * GROUP) if d else piece)
        own = pieces[0] if per_stage == 1 else jnp.concatenate(pieces, axis=0)
        across = swap(own, 2)
        keys += [own, swap(own, 1), across, swap(across, 1)]
        best = compare(s, labels, keys, best)
    backs = []
    for d in range(groups):
        back = best[:, d * cap : (d + 1) * cap]
        backs.append(swap(back, d * GROUP) if d else back)
    if per_stage > 1:
        backs = [
            jnp.concatenate(backs[s * per_stage : (s + 1) * per_stage], axis=1)
            for s in range(STAGES)
        ]
    return unpack(slot, backs).reshape(rows)


def solution(mesh):
    placed = (P(("parts", "blk"), None), P(("parts", "blk")), P(("parts", "blk")))
    return jax.shard_map(
        on_device, mesh=mesh, in_specs=placed, out_specs=P(("parts", "blk")), check_vma=False
    )
```

```python
import jax
import jax.numpy as jnp
from jax import lax
from jax.experimental import pallas as pl
from jax.experimental.pallas import tpu as pltpu
from jax.sharding import PartitionSpec as P

GROUP = 4
UNITS = (4, 4, 4, 2, 2)
NT = (((1,), (1,)), ((), ()))


def iota(shape, axis):
    return lax.broadcasted_iota(jnp.int32, shape, axis)


def spans(widths):
    start, out = 0, []
    for width in widths:
        out.append((start, width))
        start += width
    return out


def pack_kernel(groups, cap, units, pieces, emb_hbm, owner_hbm, cluster_hbm, *refs):
    blocks, refs = refs[: len(units)], refs[len(units) :]
    labels, refs = refs[: len(pieces)], refs[len(pieces) :]
    slot_ref, emb_ref, owner_ref, cluster_ref, sems = refs
    copies = [
        pltpu.make_async_copy(owner_hbm, owner_ref, sems.at[0]),
        pltpu.make_async_copy(cluster_hbm, cluster_ref, sems.at[1]),
        pltpu.make_async_copy(emb_hbm, emb_ref, sems.at[2]),
    ]
    for copy in copies:
        copy.start()
    rows = emb_ref.shape[0]
    earlier = (iota((rows, rows), 0) < iota((rows, rows), 1)).astype(jnp.bfloat16)
    mine = lax.axis_index("blk") // GROUP
    copies[0].wait()
    rel = ((owner_ref[...] >> 2) - mine + groups) & (groups - 1)
    place = jnp.where(rel > groups // 2, 2 * (groups - rel), jnp.maximum(2 * rel - 1, 0))
    member = iota((max(groups, 16), rows), 0) == place
    count = jnp.dot(member.astype(jnp.bfloat16), earlier, preferred_element_type=jnp.float32)
    rank = jnp.sum(jnp.where(member, count, 0.0), axis=0, keepdims=True)
    slot = place * cap + rank.astype(jnp.int32)
    slot_ref[...] = slot
    copies[1].wait()
    label = ((cluster_ref[...] & 15) + 1).astype(jnp.float32).astype(jnp.bfloat16)
    label = jnp.broadcast_to(label, (16, rows))
    copies[2].wait()
    x = emb_ref[...]
    squares = jnp.sum(x * x, axis=1, keepdims=True)
    unit = (x * lax.rsqrt(squares + 1e-06)).astype(jnp.bfloat16)
    for u, (start, size) in enumerate(units):
        hot = (iota((size, rows), 0) + start == slot).astype(jnp.bfloat16)
        blocks[u][...] = jnp.dot(hot, unit, preferred_element_type=jnp.float32).astype(jnp.bfloat16)
        packed = lax.dot_general(label, hot, NT, preferred_element_type=jnp.float32)
        packed = packed[0:1, :] - 1.0
        for i, (low, width) in enumerate(pieces):
            a, b = max(low, start), min(low + width, start + size)
            if a < b:
                labels[i][:, a - low : b - low] = packed[:, a - start : b - start]


def pack(groups, cap, units, pieces, embedding, owner, cluster):
    rows, width = embedding.shape
    return pl.pallas_call(
        lambda *refs: pack_kernel(groups, cap, units, pieces, *refs),
        in_specs=[pl.BlockSpec(memory_space=pl.ANY)] * 3,
        out_shape=[jax.ShapeDtypeStruct((n, width), jnp.bfloat16) for _, n in units]
        + [jax.ShapeDtypeStruct((1, n), jnp.float32) for _, n in pieces]
        + [jax.ShapeDtypeStruct((1, rows), jnp.int32)],
        scratch_shapes=[
            pltpu.VMEM((rows, width), jnp.float32),
            pltpu.VMEM((1, rows), jnp.int32),
            pltpu.VMEM((1, rows), jnp.int32),
            pltpu.SemaphoreType.DMA((3,)),
        ],
        name="pack",
    )(embedding, owner.reshape(1, rows), cluster.reshape(1, rows))


def compare_kernel(units, outs, *refs):
    last = len(units) - 1
    labels, refs = refs[:4], refs[4:]
    queries, refs = refs[: last + 1], refs[last + 1 :]
    fresh, refs = refs[:3], refs[3:]
    stacks, refs = refs[:last], refs[last:]
    if last:
        best_ref, refs = refs[0], refs[1:]
    stack_ref, out_refs = refs[0], refs[1:]
    start, size = units[last]
    for peer, ref in enumerate((queries[last],) + tuple(fresh)):
        stack_ref[peer * size : (peer + 1) * size, :] = ref[...]

    def columns(low, width):
        wide = [
            jnp.broadcast_to(labels[p][:, low : low + width], (8, width)).T[:, 0:1]
            for p in range(4)
        ]
        return jnp.concatenate(wide, axis=0)

    def block(keys, column, q, same):
        low, width = units[q]
        scores = lax.dot_general(keys, queries[q][...], NT, preferred_element_type=jnp.float32)
        allowed = column == labels[0][:, low : low + width]
        if same:
            allowed = allowed & (iota(scores.shape, 0) != iota(scores.shape, 1))
        return jnp.max(jnp.where(allowed, scores, -1.0), axis=0, keepdims=True)

    stack = stack_ref[...]
    column = columns(start, size)
    bests = []
    for q in range(last + 1):
        best = jnp.maximum(block(stack, column, q, q == last), -1.0)
        if q < last:
            low, width = units[q]
            best = jnp.maximum(best, best_ref[:, low : low + width])
        else:
            for k in range(last):
                best = jnp.maximum(best, block(stacks[k][...], columns(*units[k]), q, False))
        bests.append(best)
    for i, (low, width) in enumerate(outs):
        for q, (a, n) in enumerate(units):
            x, y = max(low, a), min(low + width, a + n)
            if x < y:
                out_refs[i][:, x - low : y - low] = bests[q][:, x - a : y - a]


def compare(units, outs, labels, queries, fresh, stacks, best):
    start, size = units[-1]
    width = queries[0].shape[1]
    pairs = 4 * size * (start + size) + 4 * start * size
    results = pl.pallas_call(
        lambda *refs: compare_kernel(units, outs, *refs),
        out_shape=[jax.ShapeDtypeStruct((4 * size, width), jnp.bfloat16)]
        + [jax.ShapeDtypeStruct((1, n), jnp.float32) for _, n in outs],
        cost_estimate=pl.CostEstimate(
            flops=2 * pairs * width,
            bytes_accessed=8 * (start + 2 * size) * width,
            transcendentals=0,
        ),
        name=f"compare{len(units)}",
    )(*labels, *queries, *fresh, *stacks, *best)
    return results[0], results[1:]


def unpack_kernel(slot_ref, *refs):
    out_ref = refs[-1]
    slot = slot_ref[...]
    rows = slot.shape[1]
    total = jnp.zeros((8, rows), jnp.float32)
    start = 0
    for ref in refs[:-1]:
        size = ref.shape[1]
        column = jnp.broadcast_to(ref[...], (8, size)).T[:, 0:1]
        hit = iota((size, rows), 0) + start == slot
        part = jnp.where(hit, column, 0.0)
        total = total + jnp.sum(part.reshape(size // 8, 8, rows), axis=0)
        start += size
    out_ref[...] = jnp.sum(total, axis=0, keepdims=True)


def unpack(slot, backs):
    return pl.pallas_call(
        unpack_kernel,
        out_shape=jax.ShapeDtypeStruct(slot.shape, jnp.float32),
        name="unpack",
    )(slot, *backs)


def join(parts, axis):
    return parts[0] if len(parts) == 1 else jnp.concatenate(parts, axis=axis)


def on_device(embedding, row_owner, cluster_id):
    rows, _ = embedding.shape
    devices = lax.axis_size("blk")
    groups = devices // GROUP
    cap = GROUP * max(2, 2 * rows // devices)
    slots = groups * cap
    units = spans([n * slots // sum(UNITS) for n in UNITS])
    pieces = spans([max(cap, 128)] * (slots // max(cap, 128)))
    shifts = [0] + [(k + 1) // 2 if k % 2 else groups - k // 2 for k in range(1, groups)]

    def shift(array, distance):
        step = distance * GROUP
        return lax.ppermute(array, "blk", [(i, (i + step) % devices) for i in range(devices)])

    def swap(array, mask):
        return lax.ppermute(array, "blk", [(i, i ^ mask) for i in range(devices)])

    def exchange(array, start, axis, sign):
        size, out = array.shape[axis], []
        for k in range(start // cap, (start + size - 1) // cap + 1):
            a, b = max(k * cap - start, 0), min((k + 1) * cap - start, size)
            part = lax.slice_in_dim(array, a, b, axis=axis)
            out.append(shift(part, sign * shifts[k]) if shifts[k] else part)
        return join(out, axis)

    sent = pack(groups, cap, units, pieces, embedding, row_owner, cluster_id)
    blocks, sent = sent[: len(units)], sent[len(units) :]
    label, slot = sent[:-1], sent[-1]
    own = join([exchange(l, low, 1, 1) for l, (low, _) in zip(label, pieces)], 1)
    across = swap(own, 2)
    labels = [own, swap(own, 1), across, swap(across, 1)]

    queries, stacks, best = [], [], []
    arrived = None
    for u, (start, size) in enumerate(units):
        block = blocks[u]
        if u >= 2:
            block, arrived = lax.optimization_barrier((block, arrived))
            queries[-1] = arrived
        arrived = exchange(block, start, 0, 1)
        queries.append(arrived)
    for u, (start, size) in enumerate(units):
        across = swap(queries[u], 2)
        fresh = [swap(queries[u], 1), across, swap(across, 1)]
        outs = pieces if u == len(units) - 1 else [(0, start + size)]
        stack, best = compare(units[: u + 1], outs, labels, queries[: u + 1], fresh, stacks, best)
        stacks.append(stack)
    backs = [exchange(b, low, 1, -1) for b, (low, _) in zip(best, pieces)]
    return unpack(slot, backs).reshape(rows)


def solution(mesh):
    placed = (P(("parts", "blk"), None), P(("parts", "blk")), P(("parts", "blk")))
    return jax.shard_map(
        on_device, mesh=mesh, in_specs=placed, out_specs=P(("parts", "blk")), check_vma=False
    )
```

```python
import jax
import jax.numpy as jnp
from jax import lax
from jax.experimental import pallas as pl
from jax.experimental.pallas import tpu as pltpu
from jax.sharding import PartitionSpec as P

GROUP = 4
UNITS = (4, 4, 4, 2, 2)
NT = (((1,), (1,)), ((), ()))


def iota(shape, axis):
    return lax.broadcasted_iota(jnp.int32, shape, axis)


def spans(widths):
    start, out = 0, []
    for width in widths:
        out.append((start, width))
        start += width
    return out


def label_kernel(groups, cap, pieces, owner_ref, cluster_ref, *refs):
    labels, slot_ref = refs[:-1], refs[-1]
    rows = owner_ref.shape[1]
    earlier = (iota((rows, rows), 0) < iota((rows, rows), 1)).astype(jnp.bfloat16)
    mine = lax.axis_index("blk") // GROUP
    rel = ((owner_ref[...] >> 2) - mine + groups) & (groups - 1)
    place = jnp.where(rel > groups // 2, 2 * (groups - rel), jnp.maximum(2 * rel - 1, 0))
    member = iota((max(groups, 16), rows), 0) == place
    count = jnp.dot(member.astype(jnp.bfloat16), earlier, preferred_element_type=jnp.float32)
    rank = jnp.sum(jnp.where(member, count, 0.0), axis=0, keepdims=True)
    slot = place * cap + rank.astype(jnp.int32)
    slot_ref[...] = slot
    label = ((cluster_ref[...] & 15) + 1).astype(jnp.float32).astype(jnp.bfloat16)
    label = jnp.broadcast_to(label, (16, rows))
    for ref, (start, size) in zip(labels, pieces):
        hot = (iota((size, rows), 0) + start == slot).astype(jnp.bfloat16)
        packed = lax.dot_general(label, hot, NT, preferred_element_type=jnp.float32)
        ref[...] = packed[0:1, :] - 1.0


def place_labels(groups, cap, pieces, owner, cluster):
    (rows,) = owner.shape
    return pl.pallas_call(
        lambda *refs: label_kernel(groups, cap, pieces, *refs),
        out_shape=[jax.ShapeDtypeStruct((1, n), jnp.float32) for _, n in pieces]
        + [jax.ShapeDtypeStruct((1, rows), jnp.int32)],
        name="labels",
    )(owner.reshape(1, rows), cluster.reshape(1, rows))


def pack_kernel(units, emb_ref, slot_ref, *blocks):
    x = emb_ref[...]
    squares = jnp.sum(x * x, axis=1, keepdims=True)
    unit = (x * lax.rsqrt(squares + 1e-06)).astype(jnp.bfloat16)
    slot = slot_ref[...]
    for ref, (start, size) in zip(blocks, units):
        hot = (iota((size, x.shape[0]), 0) + start == slot).astype(jnp.bfloat16)
        ref[...] = jnp.dot(hot, unit, preferred_element_type=jnp.float32).astype(jnp.bfloat16)


def pack(units, embedding, slot):
    width = embedding.shape[1]
    return pl.pallas_call(
        lambda *refs: pack_kernel(units, *refs),
        out_shape=[jax.ShapeDtypeStruct((n, width), jnp.bfloat16) for _, n in units],
        name="pack",
    )(embedding, slot)


def compare_kernel(units, outs, *refs):
    last = len(units) - 1
    labels, refs = refs[:4], refs[4:]
    keys, refs = refs[: 4 * last + 4], refs[4 * last + 4 :]
    if last:
        best_ref, refs = refs[0], refs[1:]
    columns = []
    for low, width in units:
        wide = jnp.concatenate([ref[:, low : low + width] for ref in labels] * 2, axis=0)
        columns.append(wide.T)

    def tile(q, k, peer, best):
        low, width = units[q]
        scores = lax.dot_general(
            keys[4 * k + peer][...], keys[4 * q][...], NT, preferred_element_type=jnp.float32
        )
        allowed = columns[k][:, peer : peer + 1] == labels[0][:, low : low + width]
        if peer == 0 and q == k:
            allowed = allowed & (iota(scores.shape, 0) != iota(scores.shape, 1))
        return jnp.maximum(best, jnp.max(jnp.where(allowed, scores, -1.0), axis=0, keepdims=True))

    bests = []
    for q, (low, width) in enumerate(units):
        best = best_ref[:, low : low + width] if q < last else jnp.full((1, width), -1.0)
        for k in range(last + 1) if q == last else [last]:
            for peer in range(4):
                best = tile(q, k, peer, best)
        bests.append(best)
    for ref, (low, width) in zip(refs, outs):
        for q, (a, n) in enumerate(units):
            x, y = max(low, a), min(low + width, a + n)
            if x < y:
                ref[:, x - low : y - low] = bests[q][:, x - a : y - a]


def compare(units, outs, labels, keys, best):
    start, size = units[-1]
    width = keys[0].shape[1]
    pairs = 4 * size * (start + size) + 4 * start * size
    return pl.pallas_call(
        lambda *refs: compare_kernel(units, outs, *refs),
        out_shape=[jax.ShapeDtypeStruct((1, n), jnp.float32) for _, n in outs],
        cost_estimate=pl.CostEstimate(
            flops=2 * pairs * width,
            bytes_accessed=8 * (start + size) * width,
            transcendentals=0,
        ),
        name=f"compare{len(units)}",
    )(*labels, *keys, *best)


def unpack_kernel(slot_ref, *refs):
    out_ref = refs[-1]
    slot = slot_ref[...]
    rows = slot.shape[1]
    total = jnp.zeros((8, rows), jnp.float32)
    start = 0
    for ref in refs[:-1]:
        size = ref.shape[1]
        column = jnp.broadcast_to(ref[...], (8, size)).T[:, 0:1]
        hit = iota((size, rows), 0) + start == slot
        part = jnp.where(hit, column, 0.0)
        total = total + jnp.sum(part.reshape(size // 8, 8, rows), axis=0)
        start += size
    out_ref[...] = jnp.sum(total, axis=0, keepdims=True)


def unpack(slot, backs):
    return pl.pallas_call(
        unpack_kernel,
        out_shape=jax.ShapeDtypeStruct(slot.shape, jnp.float32),
        name="unpack",
    )(slot, *backs)


def join(parts, axis):
    return parts[0] if len(parts) == 1 else jnp.concatenate(parts, axis=axis)


def on_device(embedding, row_owner, cluster_id):
    rows, _ = embedding.shape
    devices = lax.axis_size("blk")
    groups = devices // GROUP
    cap = GROUP * max(2, 2 * rows // devices)
    slots = groups * cap
    units = spans([n * slots // sum(UNITS) for n in UNITS])
    pieces = spans([max(cap, 128)] * (slots // max(cap, 128)))
    shifts = [0] + [(k + 1) // 2 if k % 2 else groups - k // 2 for k in range(1, groups)]

    def shift(array, distance):
        step = distance * GROUP
        return lax.ppermute(array, "blk", [(i, (i + step) % devices) for i in range(devices)])

    def swap(array, mask):
        return lax.ppermute(array, "blk", [(i, i ^ mask) for i in range(devices)])

    def exchange(array, start, axis, sign):
        size, out = array.shape[axis], []
        for k in range(start // cap, (start + size - 1) // cap + 1):
            a, b = max(k * cap - start, 0), min((k + 1) * cap - start, size)
            part = lax.slice_in_dim(array, a, b, axis=axis)
            out.append(shift(part, sign * shifts[k]) if shifts[k] else part)
        return join(out, axis)

    *label, slot = place_labels(groups, cap, pieces, row_owner, cluster_id)
    blocks = pack(units, embedding, slot)
    own = join([exchange(l, low, 1, 1) for l, (low, _) in zip(label, pieces)], 1)
    across = swap(own, 2)
    labels = [own, swap(own, 1), across, swap(across, 1)]

    queries = []
    for u, (start, _) in enumerate(units):
        block = blocks[u]
        if u == 2:
            block, labels = lax.optimization_barrier((block, labels))
        if u >= 3:
            block, queries[u - 2] = lax.optimization_barrier((block, queries[u - 2]))
        queries.append(exchange(block, start, 0, 1))
    keys, best = [], []
    for u, (start, size) in enumerate(units):
        across = swap(queries[u], 2)
        keys += [queries[u], swap(queries[u], 1), across, swap(across, 1)]
        outs = pieces if u == len(units) - 1 else [(0, start + size)]
        best = compare(units[: u + 1], outs, labels, keys, best)
    backs = [exchange(b, low, 1, -1) for b, (low, _) in zip(best, pieces)]
    return unpack(slot, backs).reshape(rows)


def solution(mesh):
    placed = (P(("parts", "blk"), None), P(("parts", "blk")), P(("parts", "blk")))
    return jax.shard_map(
        on_device, mesh=mesh, in_specs=placed, out_specs=P(("parts", "blk")), check_vma=False
    )
```

```python
import jax
import jax.numpy as jnp
from jax import lax
from jax.experimental import pallas as pl
from jax.experimental.pallas import tpu as pltpu
from jax.sharding import PartitionSpec as P

GROUP = 4
UNITS = (4, 4, 4, 2, 2)
GRANT = 16 << 20
NT = (((1,), (1,)), ((), ()))


def iota(shape, axis):
    return lax.broadcasted_iota(jnp.int32, shape, axis)


def spans(widths):
    start, out = 0, []
    for width in widths:
        out.append((start, width))
        start += width
    return out


def pack_kernel(groups, cap, units, pieces, emb_hbm, owner_hbm, cluster_hbm, *refs):
    blocks, refs = refs[: len(units)], refs[len(units) :]
    labels, refs = refs[: len(pieces)], refs[len(pieces) :]
    slot_ref, emb_ref, unit_ref, owner_ref, cluster_ref, sems = refs
    rows = emb_ref.shape[0]
    part = rows // 4
    copies = [
        pltpu.make_async_copy(owner_hbm, owner_ref, sems.at[0]),
        pltpu.make_async_copy(cluster_hbm, cluster_ref, sems.at[1]),
    ]
    for i in range(4):
        span = pl.ds(i * part, part)
        copies.append(pltpu.make_async_copy(emb_hbm.at[span], emb_ref.at[span], sems.at[2 + i]))
    for copy in copies:
        copy.start()
    earlier = (iota((rows, rows), 0) < iota((rows, rows), 1)).astype(jnp.bfloat16)
    mine = lax.axis_index("blk") // GROUP
    copies[0].wait()
    rel = ((owner_ref[...] >> 2) - mine + groups) & (groups - 1)
    place = jnp.where(rel > groups // 2, 2 * (groups - rel), jnp.maximum(2 * rel - 1, 0))
    member = iota((max(groups, 16), rows), 0) == place
    count = jnp.dot(member.astype(jnp.bfloat16), earlier, preferred_element_type=jnp.float32)
    rank = jnp.sum(jnp.where(member, count, 0.0), axis=0, keepdims=True)
    slot = place * cap + rank.astype(jnp.int32)
    slot_ref[...] = slot
    copies[1].wait()
    label = ((cluster_ref[...] & 15) + 1).astype(jnp.float32).astype(jnp.bfloat16)
    label = jnp.broadcast_to(label, (16, rows))
    for i in range(4):
        copies[2 + i].wait()
        x = emb_ref[i * part : (i + 1) * part, :]
        squares = jnp.sum(x * x, axis=1, keepdims=True)
        unit_ref[i * part : (i + 1) * part, :] = (x * lax.rsqrt(squares + 1e-06)).astype(
            jnp.bfloat16
        )
    unit = unit_ref[...]
    for u, (start, size) in enumerate(units):
        hot = (iota((size, rows), 0) + start == slot).astype(jnp.bfloat16)
        blocks[u][...] = jnp.dot(hot, unit, preferred_element_type=jnp.float32).astype(jnp.bfloat16)
        packed = lax.dot_general(label, hot, NT, preferred_element_type=jnp.float32)
        packed = packed[0:1, :] - 1.0
        for i, (low, width) in enumerate(pieces):
            a, b = max(low, start), min(low + width, start + size)
            if a < b:
                labels[i][:, a - low : b - low] = packed[:, a - start : b - start]


def pack(groups, cap, units, pieces, embedding, owner, cluster):
    rows, width = embedding.shape
    return pl.pallas_call(
        lambda *refs: pack_kernel(groups, cap, units, pieces, *refs),
        in_specs=[pl.BlockSpec(memory_space=pltpu.HBM)] * 3,
        out_shape=[jax.ShapeDtypeStruct((n, width), jnp.bfloat16) for _, n in units]
        + [jax.ShapeDtypeStruct((1, n), jnp.float32) for _, n in pieces]
        + [jax.ShapeDtypeStruct((1, rows), jnp.int32)],
        scratch_shapes=[
            pltpu.VMEM((rows, width), jnp.float32),
            pltpu.VMEM((rows, width), jnp.bfloat16),
            pltpu.VMEM((1, rows), jnp.int32),
            pltpu.VMEM((1, rows), jnp.int32),
            pltpu.SemaphoreType.DMA((6,)),
        ],
        compiler_params=pltpu.CompilerParams(vmem_limit_bytes=GRANT),
        name="pack",
    )(embedding, owner.reshape(1, rows), cluster.reshape(1, rows))


def compare_kernel(units, outs, *refs):
    last = len(units) - 1
    near, far, refs = refs[0], refs[1], refs[2:]
    keys, refs = refs[: 4 * last + 4], refs[4 * last + 4 :]
    if last:
        best_ref, refs = refs[0], refs[1:]
    outputs, query_ref = refs[:-1], refs[-1]
    for q, (low, width) in enumerate(units):
        query_ref[low : low + width, :] = keys[4 * q][...]
    columns = []
    for low, width in units:
        span = slice(low, low + width)
        wide = jnp.concatenate([near[:, span], far[:, span]] * 2, axis=0)
        columns.append(wide.T)

    def block(k, peer, low, width, same):
        scores = lax.dot_general(
            keys[4 * k + peer][...],
            query_ref[low : low + width, :],
            NT,
            preferred_element_type=jnp.float32,
        )
        allowed = columns[k][:, peer : peer + 1] == near[0:1, low : low + width]
        if same is not None:
            allowed = allowed & (iota(scores.shape, 0) + same != iota(scores.shape, 1))
        return jnp.max(jnp.where(allowed, scores, -1.0), axis=0, keepdims=True)

    start, size = units[last]
    total = start + size
    step = 256
    for low in range(0, total, step):
        width = min(step, total - low)
        best = jnp.full((1, width), -1.0)
        for peer in range(4):
            inside = peer == 0 and low <= start < low + width
            best = jnp.maximum(best, block(last, peer, low, width, start - low if inside else None))
        head = min(max(start - low, 0), width)
        if head:
            old = jnp.maximum(best[:, :head], best_ref[:, low : low + head])
            spread(outputs, outs, low, old)
        if head < width:
            new = best[:, head:]
            for k in range(last):
                for peer in range(4):
                    new = jnp.maximum(new, block(k, peer, start, size, None))
            spread(outputs, outs, start, new)


def spread(refs, outs, start, row):
    for ref, (low, width) in zip(refs, outs):
        a, b = max(low, start), min(low + width, start + row.shape[1])
        if a < b:
            ref[:, a - low : b - low] = row[:, a - start : b - start]


def compare(units, outs, labels, keys, best):
    start, size = units[-1]
    width = keys[0].shape[1]
    pairs = 4 * size * (start + size) + 4 * start * size
    return pl.pallas_call(
        lambda *refs: compare_kernel(units, outs, *refs),
        out_shape=[jax.ShapeDtypeStruct((1, n), jnp.float32) for _, n in outs],
        scratch_shapes=[pltpu.VMEM((start + size, width), jnp.bfloat16)],
        compiler_params=pltpu.CompilerParams(vmem_limit_bytes=GRANT),
        cost_estimate=pl.CostEstimate(
            flops=2 * pairs * width,
            bytes_accessed=8 * (start + size) * width,
            transcendentals=0,
        ),
        name=f"compare{len(units)}",
    )(*labels, *keys, *best)


def unpack_kernel(slot_ref, *refs):
    out_ref = refs[-1]
    slot = slot_ref[...]
    rows = slot.shape[1]
    total = jnp.zeros((8, rows), jnp.float32)
    start = 0
    for ref in refs[:-1]:
        size = ref.shape[1]
        column = jnp.broadcast_to(ref[...], (8, size)).T[:, 0:1]
        hit = iota((size, rows), 0) + start == slot
        part = jnp.where(hit, column, 0.0)
        total = total + jnp.sum(part.reshape(size // 8, 8, rows), axis=0)
        start += size
    out_ref[...] = jnp.sum(total, axis=0, keepdims=True)


def unpack(slot, backs):
    return pl.pallas_call(
        unpack_kernel,
        out_shape=jax.ShapeDtypeStruct(slot.shape, jnp.float32),
        compiler_params=pltpu.CompilerParams(vmem_limit_bytes=GRANT),
        name="unpack",
    )(slot, *backs)


def join(parts, axis):
    return parts[0] if len(parts) == 1 else jnp.concatenate(parts, axis=axis)


def on_device(embedding, row_owner, cluster_id):
    rows, _ = embedding.shape
    devices = lax.axis_size("blk")
    groups = devices // GROUP
    cap = GROUP * max(2, 2 * rows // devices)
    slots = groups * cap
    units = spans([n * slots // sum(UNITS) for n in UNITS])
    pieces = spans([max(cap, 128)] * (slots // max(cap, 128)))
    shifts = [0] + [(k + 1) // 2 if k % 2 else groups - k // 2 for k in range(1, groups)]

    def shift(array, distance):
        step = distance * GROUP
        return lax.ppermute(array, "blk", [(i, (i + step) % devices) for i in range(devices)])

    def swap(array, mask):
        return lax.ppermute(array, "blk", [(i, i ^ mask) for i in range(devices)])

    def exchange(array, start, axis, sign):
        size, out = array.shape[axis], []
        for k in range(start // cap, (start + size - 1) // cap + 1):
            a, b = max(k * cap - start, 0), min((k + 1) * cap - start, size)
            part = lax.slice_in_dim(array, a, b, axis=axis)
            out.append(shift(part, sign * shifts[k]) if shifts[k] else part)
        return join(out, axis)

    sent = pack(groups, cap, units, pieces, embedding, row_owner, cluster_id)
    blocks, label, slot = list(sent[: len(units)]), sent[len(units) : -1], sent[-1]

    def tie(*arrays):
        return lax.optimization_barrier(arrays)

    def send(u):
        return exchange(blocks[u], units[u][0], 0, 1)

    def cross(array):
        return swap(array, 2)

    def core(array):
        return swap(array, 1)

    last = len(units) - 1
    own = join([exchange(l, low, 1, 1) for l, (low, _) in zip(label, pieces)], 1)
    label_x = cross(own)
    near = jnp.concatenate([own, label_x], axis=0)
    labels = [near, core(near)]
    queries = []
    for u in range(last + 1):
        block = blocks[u]
        if u == 2:
            block, labels[1] = tie(block, labels[1])
        if u >= 3:
            block, queries[u - 2] = tie(block, queries[u - 2])
        queries.append(exchange(block, units[u][0], 0, 1))
    keys, best = [], []
    for u, (start, size) in enumerate(units):
        across = cross(queries[u])
        keys += [queries[u], across, core(queries[u]), core(across)]
        outs = pieces if u == last else [(0, start + size)]
        best = list(compare(units[: u + 1], outs, labels, keys, best))
    backs = [exchange(b, low, 1, -1) for b, (low, _) in zip(best, pieces)]
    return unpack(slot, backs).reshape(rows)


def solution(mesh):
    placed = (P(("parts", "blk"), None), P(("parts", "blk")), P(("parts", "blk")))
    return jax.shard_map(
        on_device, mesh=mesh, in_specs=placed, out_specs=P(("parts", "blk")), check_vma=False
    )
```

```python
import jax
import jax.numpy as jnp
from jax import lax
from jax.experimental import pallas as pl
from jax.experimental.pallas import tpu as pltpu
from jax.sharding import PartitionSpec as P

GROUP = 4
UNITS = (4, 4, 4, 4)
BLOCKS = 4
STEP = 512
GRANT = 16 << 20
NT = (((1,), (1,)), ((), ()))


def iota(shape, axis):
    return lax.broadcasted_iota(jnp.int32, shape, axis)


def spans(widths):
    start, out = 0, []
    for width in widths:
        out.append((start, width))
        start += width
    return out


def pack_kernel(groups, cap, units, pieces, emb_hbm, owner_hbm, cluster_hbm, *refs):
    blocks, refs = refs[: len(units)], refs[len(units) :]
    labels, refs = refs[: len(pieces)], refs[len(pieces) :]
    slot_ref, emb_ref, unit_ref, owner_ref, cluster_ref, sems = refs
    rows = emb_ref.shape[0]
    part = rows // 4
    copies = [
        pltpu.make_async_copy(owner_hbm, owner_ref, sems.at[0]),
        pltpu.make_async_copy(cluster_hbm, cluster_ref, sems.at[1]),
    ]
    for i in range(4):
        span = pl.ds(i * part, part)
        copies.append(pltpu.make_async_copy(emb_hbm.at[span], emb_ref.at[span], sems.at[2 + i]))
    for copy in copies:
        copy.start()
    earlier = (iota((rows, rows), 0) < iota((rows, rows), 1)).astype(jnp.bfloat16)
    mine = lax.axis_index("blk") // GROUP
    copies[0].wait()
    rel = ((owner_ref[...] >> 2) - mine + groups) & (groups - 1)
    place = jnp.where(rel > groups // 2, 2 * (groups - rel), jnp.maximum(2 * rel - 1, 0))
    member = iota((max(groups, 16), rows), 0) == place
    count = jnp.dot(member.astype(jnp.bfloat16), earlier, preferred_element_type=jnp.float32)
    rank = jnp.sum(jnp.where(member, count, 0.0), axis=0, keepdims=True)
    slot = place * cap + rank.astype(jnp.int32)
    slot_ref[...] = slot
    copies[1].wait()
    label = ((cluster_ref[...] & 15) + 1).astype(jnp.float32).astype(jnp.bfloat16)
    label = jnp.broadcast_to(label, (16, rows))
    for i in range(4):
        copies[2 + i].wait()
        x = emb_ref[i * part : (i + 1) * part, :]
        squares = jnp.sum(x * x, axis=1, keepdims=True)
        unit_ref[i * part : (i + 1) * part, :] = (x * lax.rsqrt(squares + 1e-06)).astype(
            jnp.bfloat16
        )
    unit = unit_ref[...]
    for u, (start, size) in enumerate(units):
        hot = (iota((size, rows), 0) + start == slot).astype(jnp.bfloat16)
        blocks[u][...] = jnp.dot(hot, unit, preferred_element_type=jnp.float32).astype(jnp.bfloat16)
        packed = lax.dot_general(label, hot, NT, preferred_element_type=jnp.float32)
        packed = packed[0:1, :] - 1.0
        for i, (low, width) in enumerate(pieces):
            a, b = max(low, start), min(low + width, start + size)
            if a < b:
                labels[i][:, a - low : b - low] = packed[:, a - start : b - start]


def pack(groups, cap, units, pieces, embedding, owner, cluster):
    rows, width = embedding.shape
    return pl.pallas_call(
        lambda *refs: pack_kernel(groups, cap, units, pieces, *refs),
        in_specs=[pl.BlockSpec(memory_space=pltpu.HBM)] * 3,
        out_shape=[jax.ShapeDtypeStruct((n, width), jnp.bfloat16) for _, n in units]
        + [jax.ShapeDtypeStruct((1, n), jnp.float32) for _, n in pieces]
        + [jax.ShapeDtypeStruct((1, rows), jnp.int32)],
        scratch_shapes=[
            pltpu.VMEM((rows, width), jnp.float32),
            pltpu.VMEM((rows, width), jnp.bfloat16),
            pltpu.VMEM((1, rows), jnp.int32),
            pltpu.VMEM((1, rows), jnp.int32),
            pltpu.SemaphoreType.DMA((6,)),
        ],
        name="pack",
    )(embedding, owner.reshape(1, rows), cluster.reshape(1, rows))


def compare_kernel(size, outs, jobs, shape, *refs):
    near, far, best_ref, refs = refs[0], refs[1], refs[2], refs[3:]
    count = sum(shape.values())
    pieces, refs = refs[:count], refs[count:]
    outputs, scratch = refs[: len(outs)], refs[len(outs) :]
    place = {}
    for index, key in enumerate(shape):
        start = sum(list(shape.values())[:index])
        low = 0
        for ref in pieces[start : start + shape[key]]:
            place.setdefault(key, []).append((low, ref))
            low += ref.shape[0]
    query_ref, extra = scratch[0], list(scratch[1:])
    own = [k for p, k in shape if p == 0]
    for k in own:
        for low, ref in place[0, k]:
            query_ref[k * size + low : k * size + low + ref.shape[0], :] = ref[...]
    keys = {}
    for key, parts in place.items():
        if key[0] == 0:
            keys[key] = query_ref.at[key[1] * size : (key[1] + 1) * size]
        elif len(parts) == 1:
            keys[key] = parts[0][1]
        else:
            keys[key] = extra.pop()
            for low, ref in parts:
                keys[key][low : low + ref.shape[0], :] = ref[...]
    table = jnp.concatenate([near[...], far[...]] * 2, axis=0)
    columns = {k: table[:, k * size : (k + 1) * size].T for k in sorted({k for _, k in shape})}
    bests = [best_ref[:, k * size : (k + 1) * size] for k in range(BLOCKS)]
    for low, high, k, peers in jobs:
        for left in range(low, high, STEP // size):
            right = min(left + STEP // size, high)
            span = slice(left * size, right * size)
            row = near[0:1, span]
            best = None
            for peer in peers:
                scores = lax.dot_general(
                    keys[peer, k][...],
                    query_ref[span, :],
                    NT,
                    preferred_element_type=jnp.float32,
                )
                allowed = columns[k][:, peer : peer + 1] == row
                if peer == 0 and left <= k < right:
                    shift = (k - left) * size
                    allowed = allowed & (iota(scores.shape, 0) + shift != iota(scores.shape, 1))
                top = jnp.max(jnp.where(allowed, scores, -1.0), axis=0, keepdims=True)
                best = top if best is None else jnp.maximum(best, top)
            for q in range(left, right):
                part = best[:, (q - left) * size : (q - left + 1) * size]
                bests[q] = jnp.maximum(bests[q], part)
    for q in range(BLOCKS):
        spread(outputs, outs, q * size, bests[q])


def spread(refs, outs, start, row):
    for ref, (low, width) in zip(refs, outs):
        a, b = max(low, start), min(low + width, start + row.shape[1])
        if a < b:
            ref[:, a - low : b - low] = row[:, a - start : b - start]


def compare(outs, jobs, labels, blocks, best):
    size = sum(part.shape[0] for part in blocks[0, 0])
    width = blocks[0, 0][0].shape[1]
    shape = {key: len(parts) for key, parts in blocks.items()}
    split = [key for key in shape if key[0] and shape[key] > 1]
    tiles = sum((high - low) * len(peers) for low, high, _, peers in jobs)
    queries = 1 + max(k for p, k in shape if p == 0)
    return pl.pallas_call(
        lambda *refs: compare_kernel(size, outs, jobs, shape, *refs),
        out_shape=[jax.ShapeDtypeStruct((1, n), jnp.float32) for _, n in outs],
        scratch_shapes=[pltpu.VMEM((queries * size, width), jnp.bfloat16)]
        + [pltpu.VMEM((size, width), jnp.bfloat16)] * len(split),
        compiler_params=pltpu.CompilerParams(vmem_limit_bytes=GRANT),
        cost_estimate=pl.CostEstimate(
            flops=2 * tiles * size * size * width, bytes_accessed=0, transcendentals=0
        ),
        name=f"compare{len(jobs)}_{tiles}",
    )(*labels, best, *[part for parts in blocks.values() for part in parts])


def unpack_kernel(slot_ref, *refs):
    out_ref = refs[-1]
    slot = slot_ref[...]
    rows = slot.shape[1]
    total = jnp.zeros((8, rows), jnp.float32)
    start = 0
    for ref in refs[:-1]:
        size = ref.shape[1]
        column = jnp.broadcast_to(ref[...], (8, size)).T[:, 0:1]
        hit = iota((size, rows), 0) + start == slot
        part = jnp.where(hit, column, 0.0)
        total = total + jnp.sum(part.reshape(size // 8, 8, rows), axis=0)
        start += size
    out_ref[...] = jnp.sum(total, axis=0, keepdims=True)


def unpack(slot, backs):
    return pl.pallas_call(
        unpack_kernel,
        out_shape=jax.ShapeDtypeStruct(slot.shape, jnp.float32),
        compiler_params=pltpu.CompilerParams(vmem_limit_bytes=GRANT),
        name="unpack",
    )(slot, *backs)


def join(parts, axis):
    return parts[0] if len(parts) == 1 else jnp.concatenate(parts, axis=axis)


def on_device(embedding, row_owner, cluster_id):
    rows, _ = embedding.shape
    devices = lax.axis_size("blk")
    groups = devices // GROUP
    cap = GROUP * max(2, 2 * rows // devices)
    slots = groups * cap
    units = spans([n * slots // sum(UNITS) for n in UNITS])
    pieces = spans([max(cap, 128)] * (slots // max(cap, 128)))
    shifts = [0] + [(k + 1) // 2 if k % 2 else groups - k // 2 for k in range(1, groups)]

    def shift(array, distance):
        step = distance * GROUP
        return lax.ppermute(array, "blk", [(i, (i + step) % devices) for i in range(devices)])

    def swap(array, mask):
        return lax.ppermute(array, "blk", [(i, i ^ mask) for i in range(devices)])

    def exchange(array, start, axis, sign):
        size, out = array.shape[axis], []
        for k in range(start // cap, (start + size - 1) // cap + 1):
            a, b = max(k * cap - start, 0), min((k + 1) * cap - start, size)
            part = lax.slice_in_dim(array, a, b, axis=axis)
            out.append(shift(part, sign * shifts[k]) if shifts[k] else part)
        return join(out, axis)

    sent = pack(groups, cap, units, pieces, embedding, row_owner, cluster_id)
    blocks, label, slot = list(sent[: len(units)]), sent[len(units) : -1], sent[-1]

    def tie(*arrays):
        return lax.optimization_barrier(arrays)

    def send(u):
        return exchange(blocks[u], units[u][0], 0, 1)

    def cross(array):
        return swap(array, 2)

    def core(array):
        return swap(array, 1)

    across, beside, beyond = [None] * BLOCKS, [None] * BLOCKS, [None] * BLOCKS
    own = [blocks[0], send(1), None, None]
    across[0], beside[0] = cross(own[0]), core(own[0])
    *label, beside[0] = tie(*label, beside[0])
    label = [exchange(l, low, 1, 1) for l, (low, _) in zip(label, pieces)]
    label = join(label, 1)
    near = jnp.concatenate([label, cross(label)], axis=0)
    labels = [near, core(near)]
    blocks[2], beside[0] = tie(blocks[2], beside[0])
    own[2] = send(2)
    blocks[3], own[1] = tie(blocks[3], own[1])
    own[3] = send(3)
    for u in range(1, BLOCKS):
        beside[u] = core(own[u])
        across[u] = cross(own[u])
    for u in range(BLOCKS - 1):
        beyond[u] = core(across[u])
    arrays = [own, across, beside, beyond]

    def given(peers, blocks):
        return {(peer, k): [arrays[peer][k]] for peer in peers for k in blocks}

    every, row = (0, 1, 2, 3), [(0, slots)]
    best = jnp.full((1, slots), -1.0, jnp.float32)
    jobs = [(0, 4, 0, every), (0, 4, 1, every), (0, 4, 2, (0, 2)), (0, 4, 3, (0, 2))]
    some = given((0, 2), range(4)) | given((1, 3), range(2))
    (best,) = compare(row, jobs, labels, some, best)
    across[3], best = tie(across[3], best)
    beyond[3] = core(across[3])
    some = given((0,), range(4)) | given((1, 3), (2,))
    (best,) = compare(row, [(0, 4, 2, (1, 3))], labels, some, best)
    some = given((0,), range(4)) | given((1, 3), (3,))
    best = compare(pieces, [(0, 4, 3, (1, 3))], labels, some, best)
    backs = [exchange(b, low, 1, -1) for b, (low, _) in zip(best, pieces)]
    return unpack(slot, backs).reshape(rows)


def solution(mesh):
    placed = (P(("parts", "blk"), None), P(("parts", "blk")), P(("parts", "blk")))
    return jax.shard_map(
        on_device, mesh=mesh, in_specs=placed, out_specs=P(("parts", "blk")), check_vma=False
    )
```

```python
import jax
import jax.numpy as jnp
from jax import lax
from jax.experimental import pallas as pl
from jax.experimental.pallas import tpu as pltpu
from jax.sharding import PartitionSpec as P

GROUP = 4
UNITS = (4, 4, 4, 4)
BLOCKS = 4
STEP = 512
GRANT = 16 << 20
NT = (((1,), (1,)), ((), ()))


def iota(shape, axis):
    return lax.broadcasted_iota(jnp.int32, shape, axis)


def spans(widths):
    start, out = 0, []
    for width in widths:
        out.append((start, width))
        start += width
    return out


def pack_kernel(groups, cap, units, pieces, emb_hbm, owner_hbm, cluster_hbm, *refs):
    blocks, refs = refs[: len(units)], refs[len(units) :]
    labels, refs = refs[: len(pieces)], refs[len(pieces) :]
    slot_ref, emb_ref, unit_ref, owner_ref, cluster_ref, sems = refs
    rows = emb_ref.shape[0]
    part = rows // 4
    copies = [
        pltpu.make_async_copy(owner_hbm, owner_ref, sems.at[0]),
        pltpu.make_async_copy(cluster_hbm, cluster_ref, sems.at[1]),
    ]
    for i in range(4):
        span = pl.ds(i * part, part)
        copies.append(pltpu.make_async_copy(emb_hbm.at[span], emb_ref.at[span], sems.at[2 + i]))
    for copy in copies:
        copy.start()
    earlier = (iota((rows, rows), 0) < iota((rows, rows), 1)).astype(jnp.bfloat16)
    mine = lax.axis_index("blk") // GROUP
    copies[0].wait()
    rel = ((owner_ref[...] >> 2) - mine + groups) & (groups - 1)
    place = jnp.where(rel > groups // 2, 2 * (groups - rel), jnp.maximum(2 * rel - 1, 0))
    member = iota((max(groups, 16), rows), 0) == place
    count = jnp.dot(member.astype(jnp.bfloat16), earlier, preferred_element_type=jnp.float32)
    rank = jnp.sum(jnp.where(member, count, 0.0), axis=0, keepdims=True)
    slot = place * cap + rank.astype(jnp.int32)
    slot_ref[...] = slot
    copies[1].wait()
    label = ((cluster_ref[...] & 15) + 1).astype(jnp.float32).astype(jnp.bfloat16)
    label = jnp.broadcast_to(label, (16, rows))
    for i in range(4):
        copies[2 + i].wait()
        x = emb_ref[i * part : (i + 1) * part, :]
        squares = jnp.sum(x * x, axis=1, keepdims=True)
        unit_ref[i * part : (i + 1) * part, :] = (x * lax.rsqrt(squares + 1e-06)).astype(
            jnp.bfloat16
        )
    unit = unit_ref[...]
    for u, (start, size) in enumerate(units):
        hot = (iota((size, rows), 0) + start == slot).astype(jnp.bfloat16)
        blocks[u][...] = jnp.dot(hot, unit, preferred_element_type=jnp.float32).astype(jnp.bfloat16)
        packed = lax.dot_general(label, hot, NT, preferred_element_type=jnp.float32)
        packed = packed[0:1, :] - 1.0
        for i, (low, width) in enumerate(pieces):
            a, b = max(low, start), min(low + width, start + size)
            if a < b:
                labels[i][:, a - low : b - low] = packed[:, a - start : b - start]


def pack(groups, cap, units, pieces, embedding, owner, cluster):
    rows, width = embedding.shape
    return pl.pallas_call(
        lambda *refs: pack_kernel(groups, cap, units, pieces, *refs),
        in_specs=[pl.BlockSpec(memory_space=pltpu.HBM)] * 3,
        out_shape=[jax.ShapeDtypeStruct((n, width), jnp.bfloat16) for _, n in units]
        + [jax.ShapeDtypeStruct((1, n), jnp.float32) for _, n in pieces]
        + [jax.ShapeDtypeStruct((1, rows), jnp.int32)],
        scratch_shapes=[
            pltpu.VMEM((rows, width), jnp.float32),
            pltpu.VMEM((rows, width), jnp.bfloat16),
            pltpu.VMEM((1, rows), jnp.int32),
            pltpu.VMEM((1, rows), jnp.int32),
            pltpu.SemaphoreType.DMA((6,)),
        ],
        name="pack",
    )(embedding, owner.reshape(1, rows), cluster.reshape(1, rows))


def compare_kernel(size, outs, jobs, shape, *refs):
    near, best_ref, refs = refs[0], refs[1], refs[2:]
    count = sum(shape.values())
    pieces, refs = refs[:count], refs[count:]
    outputs, scratch = refs[: len(outs)], refs[len(outs) :]
    place = {}
    for index, key in enumerate(shape):
        start = sum(list(shape.values())[:index])
        low = 0
        for ref in pieces[start : start + shape[key]]:
            place.setdefault(key, []).append((low, ref))
            low += ref.shape[0]
    query_ref, extra = scratch[0], list(scratch[1:])
    own = [k for p, k in shape if p == 0]
    for k in own:
        for low, ref in place[0, k]:
            query_ref[k * size + low : k * size + low + ref.shape[0], :] = ref[...]
    keys = {}
    for key, parts in place.items():
        if key[0] == 0:
            keys[key] = query_ref.at[key[1] * size : (key[1] + 1) * size]
        elif len(parts) == 1:
            keys[key] = parts[0][1]
        else:
            keys[key] = extra.pop()
            for low, ref in parts:
                keys[key][low : low + ref.shape[0], :] = ref[...]
    table = jnp.concatenate([near[...]] * 2, axis=0)
    columns = {k: table[:, k * size : (k + 1) * size].T for k in sorted({k for _, k in shape})}
    bests = [best_ref[:, k * size : (k + 1) * size] for k in range(BLOCKS)]
    for low, high, k, peers in jobs:
        for left in range(low, high, STEP // size):
            right = min(left + STEP // size, high)
            span = slice(left * size, right * size)
            row = near[0:1, span]
            best = None
            for peer in peers:
                scores = lax.dot_general(
                    keys[peer, k][...],
                    query_ref[span, :],
                    NT,
                    preferred_element_type=jnp.float32,
                )
                allowed = columns[k][:, peer : peer + 1] == row
                if peer == 0 and left <= k < right:
                    shift = (k - left) * size
                    allowed = allowed & (iota(scores.shape, 0) + shift != iota(scores.shape, 1))
                top = jnp.max(jnp.where(allowed, scores, -1.0), axis=0, keepdims=True)
                best = top if best is None else jnp.maximum(best, top)
            for q in range(left, right):
                part = best[:, (q - left) * size : (q - left + 1) * size]
                bests[q] = jnp.maximum(bests[q], part)
    for q in range(BLOCKS):
        spread(outputs, outs, q * size, bests[q])


def spread(refs, outs, start, row):
    for ref, (low, width) in zip(refs, outs):
        a, b = max(low, start), min(low + width, start + row.shape[1])
        if a < b:
            ref[:, a - low : b - low] = row[:, a - start : b - start]


def compare(outs, jobs, labels, blocks, best):
    size = sum(part.shape[0] for part in blocks[0, 0])
    width = blocks[0, 0][0].shape[1]
    shape = {key: len(parts) for key, parts in blocks.items()}
    split = [key for key in shape if key[0] and shape[key] > 1]
    tiles = sum((high - low) * len(peers) for low, high, _, peers in jobs)
    queries = 1 + max(k for p, k in shape if p == 0)
    return pl.pallas_call(
        lambda *refs: compare_kernel(size, outs, jobs, shape, *refs),
        out_shape=[jax.ShapeDtypeStruct((1, n), jnp.float32) for _, n in outs],
        scratch_shapes=[pltpu.VMEM((queries * size, width), jnp.bfloat16)]
        + [pltpu.VMEM((size, width), jnp.bfloat16)] * len(split),
        compiler_params=pltpu.CompilerParams(vmem_limit_bytes=GRANT),
        cost_estimate=pl.CostEstimate(
            flops=2 * tiles * size * size * width, bytes_accessed=0, transcendentals=0
        ),
        name=f"compare{len(jobs)}_{tiles}",
    )(labels, best, *[part for parts in blocks.values() for part in parts])


def unpack_kernel(slot_ref, *refs):
    out_ref = refs[-1]
    slot = slot_ref[...]
    rows = slot.shape[1]
    total = jnp.zeros((8, rows), jnp.float32)
    start = 0
    for ref in refs[:-1]:
        size = ref.shape[1]
        column = jnp.broadcast_to(ref[...], (8, size)).T[:, 0:1]
        hit = iota((size, rows), 0) + start == slot
        part = jnp.where(hit, column, 0.0)
        total = total + jnp.sum(part.reshape(size // 8, 8, rows), axis=0)
        start += size
    out_ref[...] = jnp.sum(total, axis=0, keepdims=True)


def unpack(slot, backs):
    return pl.pallas_call(
        unpack_kernel,
        out_shape=jax.ShapeDtypeStruct(slot.shape, jnp.float32),
        compiler_params=pltpu.CompilerParams(vmem_limit_bytes=GRANT),
        name="unpack",
    )(slot, *backs)


def join(parts, axis):
    return parts[0] if len(parts) == 1 else jnp.concatenate(parts, axis=axis)


def on_device(embedding, row_owner, cluster_id):
    rows, _ = embedding.shape
    devices = lax.axis_size("blk")
    groups = devices // GROUP
    cap = GROUP * max(2, 2 * rows // devices)
    slots = groups * cap
    units = spans([n * slots // sum(UNITS) for n in UNITS])
    pieces = spans([max(cap, 128)] * (slots // max(cap, 128)))
    shifts = [0] + [(k + 1) // 2 if k % 2 else groups - k // 2 for k in range(1, groups)]

    def shift(array, distance):
        step = distance * GROUP
        return lax.ppermute(array, "blk", [(i, (i + step) % devices) for i in range(devices)])

    def swap(array, mask):
        return lax.ppermute(array, "blk", [(i, i ^ mask) for i in range(devices)])

    def exchange(array, start, axis, sign):
        size, out = array.shape[axis], []
        for k in range(start // cap, (start + size - 1) // cap + 1):
            a, b = max(k * cap - start, 0), min((k + 1) * cap - start, size)
            part = lax.slice_in_dim(array, a, b, axis=axis)
            out.append(shift(part, sign * shifts[k]) if shifts[k] else part)
        return join(out, axis)

    sent = pack(groups, cap, units, [(0, slots)], embedding, row_owner, cluster_id)
    blocks, label, slot = list(sent[: len(units)]), sent[len(units) : -1], sent[-1]

    def tie(*arrays):
        return lax.optimization_barrier(arrays)

    def send(u):
        return exchange(blocks[u], units[u][0], 0, 1)

    def cross(array):
        return swap(array, 2)

    def core(array):
        return swap(array, 1)

    arrays = [[None] * BLOCKS for _ in range(4)]
    own, across, beside, beyond = arrays

    def both(function, parts):
        return [function(part) for part in parts]

    (label,) = label
    near = jnp.concatenate([label, cross(label)], axis=0)
    label = jnp.concatenate([near, core(near)], axis=0)
    blocks[0], label = tie(blocks[0], label)
    blocks[2], label = tie(blocks[2], label)
    own[0], own[1], own[2] = [blocks[0]], [send(1)], [send(2)]
    across[0], beside[0] = both(cross, own[0]), both(core, own[0])
    label = exchange(label, 0, 1, 1)
    blocks[3], label = tie(blocks[3], label)
    blocks[3], *own[1] = tie(blocks[3], *own[1])
    own[3] = [send(3)]
    for u in range(1, BLOCKS):
        beside[u], across[u] = both(core, own[u]), both(cross, own[u])
    for u in range(BLOCKS - 1):
        beyond[u] = both(core, across[u])

    def given(peers, blocks):
        return {(peer, k): arrays[peer][k] for peer in peers for k in blocks}

    every, row = (0, 1, 2, 3), [(0, slots)]
    best = jnp.full((1, slots), -1.0, jnp.float32)
    jobs = [(0, 4, 0, every), (0, 4, 1, every), (0, 4, 2, (0, 2)), (0, 4, 3, (0, 2))]
    some = given((0, 2), range(4)) | given((1, 3), range(2))
    (best,) = compare(row, jobs, label, some, best)
    across[3][0], best = tie(across[3][0], best)
    beyond[3] = both(core, across[3])
    some = given((0,), range(4)) | given((1, 3), (2,))
    (best,) = compare(row, [(0, 4, 2, (1, 3))], label, some, best)
    some = given((0,), range(4)) | given((1, 3), (3,))
    best = compare(pieces, [(0, 4, 3, (1, 3))], label, some, best)
    backs = [exchange(b, low, 1, -1) for b, (low, _) in zip(best, pieces)]
    return unpack(slot, backs).reshape(rows)


def solution(mesh):
    placed = (P(("parts", "blk"), None), P(("parts", "blk")), P(("parts", "blk")))
    return jax.shard_map(
        on_device, mesh=mesh, in_specs=placed, out_specs=P(("parts", "blk")), check_vma=False
    )
```

```python
import jax
import jax.numpy as jnp
from jax import lax
from jax.experimental import pallas as pl
from jax.experimental.pallas import tpu as pltpu
from jax.sharding import PartitionSpec as P

GROUP = 4
BLOCKS = 4
PAD = 16
STEP = 512
GRANT = 16 << 20
NT = (((1,), (1,)), ((), ()))


def iota(shape, axis):
    return lax.broadcasted_iota(jnp.int32, shape, axis)


def spans(widths):
    start, out = 0, []
    for width in widths:
        out.append((start, width))
        start += width
    return out


def pack_kernel(groups, cap, units, emb_hbm, owner_hbm, cluster_hbm, *refs):
    blocks, refs = refs[: len(units)], refs[len(units) :]
    slot_ref, emb_ref, unit_ref, owner_ref, cluster_ref, sems = refs
    rows = emb_ref.shape[0]
    part = rows // 4
    copies = [
        pltpu.make_async_copy(owner_hbm, owner_ref, sems.at[0]),
        pltpu.make_async_copy(cluster_hbm, cluster_ref, sems.at[1]),
    ]
    for i in range(4):
        span = pl.ds(i * part, part)
        copies.append(pltpu.make_async_copy(emb_hbm.at[span], emb_ref.at[span], sems.at[2 + i]))
    for copy in copies:
        copy.start()
    earlier = (iota((rows, rows), 0) < iota((rows, rows), 1)).astype(jnp.bfloat16)
    mine = lax.axis_index("blk") // GROUP
    copies[0].wait()
    rel = ((owner_ref[...] >> 2) - mine + groups) & (groups - 1)
    place = jnp.where(rel > groups // 2, 2 * (groups - rel), jnp.maximum(2 * rel - 1, 0))
    member = iota((max(groups, 16), rows), 0) == place
    count = jnp.dot(member.astype(jnp.bfloat16), earlier, preferred_element_type=jnp.float32)
    rank = jnp.sum(jnp.where(member, count, 0.0), axis=0, keepdims=True)
    slot = place * cap + rank.astype(jnp.int32)
    slot_ref[...] = slot
    copies[1].wait()
    label = ((cluster_ref[...] & 15) + 1).astype(jnp.float32).astype(jnp.bfloat16)
    label = jnp.broadcast_to(label, (PAD, rows))
    for i in range(4):
        copies[2 + i].wait()
        x = emb_ref[i * part : (i + 1) * part, :]
        squares = jnp.sum(x * x, axis=1, keepdims=True)
        unit_ref[i * part : (i + 1) * part, :] = (x * lax.rsqrt(squares + 1e-06)).astype(
            jnp.bfloat16
        )
    unit = unit_ref[...]
    for ref, (start, size) in zip(blocks, units):
        hot = (iota((size, rows), 0) + start == slot).astype(jnp.bfloat16)
        packed = jnp.dot(hot, unit, preferred_element_type=jnp.float32).astype(jnp.bfloat16)
        marks = lax.dot_general(label, hot, NT, preferred_element_type=jnp.float32)
        marks = (marks - 1.0).astype(jnp.bfloat16)
        for i in range(size // cap):
            low = i * (cap + PAD)
            ref[low : low + cap, :] = packed[i * cap : (i + 1) * cap, :]
            ref[low + cap : low + cap + PAD, :] = jnp.zeros((PAD, unit.shape[1]), jnp.bfloat16)
            ref[low + cap : low + cap + PAD, 0:cap] = marks[:, i * cap : (i + 1) * cap]


def pack(groups, cap, units, embedding, owner, cluster):
    rows, width = embedding.shape
    return pl.pallas_call(
        lambda *refs: pack_kernel(groups, cap, units, *refs),
        in_specs=[pl.BlockSpec(memory_space=pltpu.HBM)] * 3,
        out_shape=[
            jax.ShapeDtypeStruct((n // cap * (cap + PAD), width), jnp.bfloat16) for _, n in units
        ]
        + [jax.ShapeDtypeStruct((1, rows), jnp.int32)],
        scratch_shapes=[
            pltpu.VMEM((rows, width), jnp.float32),
            pltpu.VMEM((rows, width), jnp.bfloat16),
            pltpu.VMEM((1, rows), jnp.int32),
            pltpu.VMEM((1, rows), jnp.int32),
            pltpu.SemaphoreType.DMA((6,)),
        ],
        name="pack",
    )(embedding, owner.reshape(1, rows), cluster.reshape(1, rows))


def compare_kernel(cap, outs, jobs, names, *refs):
    best_ref, refs = refs[0], refs[1:]
    given, refs = dict(zip(names, refs)), refs[len(names) :]
    outputs, scratch = refs[: len(outs)], list(refs[len(outs) :])
    query_ref = scratch.pop()
    size = query_ref.shape[0] // BLOCKS

    def unfold(ref, target, low):
        for i in range(size // cap):
            start = i * (cap + PAD)
            target[low + i * cap : low + (i + 1) * cap, :] = ref[start : start + cap, :]

    keys, marks = {}, {}
    for (peer, k), ref in given.items():
        parts = []
        for i in range(size // cap):
            start = i * (cap + PAD) + cap
            parts.append(ref[start : start + PAD, 0:cap].astype(jnp.float32))
        marks[peer, k] = jnp.concatenate(parts, axis=1)[0:1, :]
        if peer == 0:
            unfold(ref, query_ref, k * size)
            keys[peer, k] = query_ref.at[k * size : (k + 1) * size]
        elif size == cap:
            keys[peer, k] = ref.at[0:cap]
        else:
            keys[peer, k] = scratch.pop()
            unfold(ref, keys[peer, k], 0)
    columns = {}
    for k in range(BLOCKS):
        table = [marks.get((peer, k), marks[0, k]) for peer in range(4)]
        columns[k] = jnp.concatenate(table * 2, axis=0).T
    near = jnp.concatenate([marks[0, k] for k in range(BLOCKS)], axis=1)
    bests = [best_ref[:, k * size : (k + 1) * size] for k in range(BLOCKS)]
    for low, high, k, peers in jobs:
        for left in range(low, high, STEP // size):
            right = min(left + STEP // size, high)
            span = slice(left * size, right * size)
            row = near[0:1, span]
            best = None
            for peer in peers:
                scores = lax.dot_general(
                    keys[peer, k][...],
                    query_ref[span, :],
                    NT,
                    preferred_element_type=jnp.float32,
                )
                allowed = columns[k][:, peer : peer + 1] == row
                if peer == 0 and left <= k < right:
                    shift = (k - left) * size
                    allowed = allowed & (iota(scores.shape, 0) + shift != iota(scores.shape, 1))
                top = jnp.max(jnp.where(allowed, scores, -1.0), axis=0, keepdims=True)
                best = top if best is None else jnp.maximum(best, top)
            for q in range(left, right):
                part = best[:, (q - left) * size : (q - left + 1) * size]
                bests[q] = jnp.maximum(bests[q], part)
    for q in range(BLOCKS):
        spread(outputs, outs, q * size, bests[q])


def spread(refs, outs, start, row):
    for ref, (low, width) in zip(refs, outs):
        a, b = max(low, start), min(low + width, start + row.shape[1])
        if a < b:
            ref[:, a - low : b - low] = row[:, a - start : b - start]


def compare(cap, outs, jobs, blocks, best):
    slots, width = best.shape[1], blocks[0, 0].shape[1]
    size = slots // BLOCKS
    tiles = sum((high - low) * len(peers) for low, high, _, peers in jobs)
    folded = sum(1 for peer, _ in blocks if peer) if size > cap else 0
    return pl.pallas_call(
        lambda *refs: compare_kernel(cap, outs, jobs, tuple(blocks), *refs),
        out_shape=[jax.ShapeDtypeStruct((1, n), jnp.float32) for _, n in outs],
        scratch_shapes=[pltpu.VMEM((size, width), jnp.bfloat16)] * folded
        + [pltpu.VMEM((slots, width), jnp.bfloat16)],
        compiler_params=pltpu.CompilerParams(vmem_limit_bytes=GRANT),
        cost_estimate=pl.CostEstimate(
            flops=2 * tiles * size * size * width, bytes_accessed=0, transcendentals=0
        ),
        name=f"compare{len(jobs)}_{tiles}",
    )(best, *blocks.values())


def unpack_kernel(slot_ref, *refs):
    out_ref = refs[-1]
    slot = slot_ref[...]
    rows = slot.shape[1]
    total = jnp.zeros((8, rows), jnp.float32)
    start = 0
    for ref in refs[:-1]:
        size = ref.shape[1]
        column = jnp.broadcast_to(ref[...], (8, size)).T[:, 0:1]
        hit = iota((size, rows), 0) + start == slot
        part = jnp.where(hit, column, 0.0)
        total = total + jnp.sum(part.reshape(size // 8, 8, rows), axis=0)
        start += size
    out_ref[...] = jnp.sum(total, axis=0, keepdims=True)


def unpack(slot, backs):
    return pl.pallas_call(
        unpack_kernel,
        out_shape=jax.ShapeDtypeStruct(slot.shape, jnp.float32),
        compiler_params=pltpu.CompilerParams(vmem_limit_bytes=GRANT),
        name="unpack",
    )(slot, *backs)


def join(parts, axis):
    return parts[0] if len(parts) == 1 else jnp.concatenate(parts, axis=axis)


def on_device(embedding, row_owner, cluster_id):
    rows, _ = embedding.shape
    devices = lax.axis_size("blk")
    groups = devices // GROUP
    cap = GROUP * max(2, 2 * rows // devices)
    slots = groups * cap
    units = spans([slots // BLOCKS] * BLOCKS)
    pieces = spans([max(cap, 128)] * (slots // max(cap, 128)))
    shifts = [0] + [(k + 1) // 2 if k % 2 else groups - k // 2 for k in range(1, groups)]

    def shift(array, distance):
        step = distance * GROUP
        return lax.ppermute(array, "blk", [(i, (i + step) % devices) for i in range(devices)])

    def swap(array, mask):
        return lax.ppermute(array, "blk", [(i, i ^ mask) for i in range(devices)])

    def exchange(array, start, axis, sign):
        size, out = array.shape[axis], []
        for k in range(start // cap, (start + size - 1) // cap + 1):
            a, b = max(k * cap - start, 0), min((k + 1) * cap - start, size)
            part = lax.slice_in_dim(array, a, b, axis=axis)
            out.append(shift(part, sign * shifts[k]) if shifts[k] else part)
        return join(out, axis)

    *blocks, slot = pack(groups, cap, units, embedding, row_owner, cluster_id)

    def tie(*arrays):
        return lax.optimization_barrier(arrays)

    def send(u):
        array, out = blocks[u], []
        for i in range(array.shape[0] // (cap + PAD)):
            part = lax.slice_in_dim(array, i * (cap + PAD), (i + 1) * (cap + PAD))
            distance = shifts[units[u][0] // cap + i]
            out.append(shift(part, distance) if distance else part)
        return join(out, 0)

    def cross(array):
        return swap(array, 2)

    def core(array):
        return swap(array, 1)

    arrays = [[None] * BLOCKS for _ in range(4)]
    own, across, beside, beyond = arrays
    own[0], own[1] = blocks[0], send(1)
    across[0], beside[0] = cross(own[0]), core(own[0])
    blocks[2], beside[0] = tie(blocks[2], beside[0])
    own[2] = send(2)
    blocks[3], own[1] = tie(blocks[3], own[1])
    own[3] = send(3)
    for u in range(1, BLOCKS):
        beside[u] = core(own[u])
        across[u] = cross(own[u])
    for u in range(BLOCKS - 1):
        beyond[u] = core(across[u])

    def given(peers, blocks):
        return {(peer, k): arrays[peer][k] for peer in peers for k in blocks}

    every, row = (0, 1, 2, 3), [(0, slots)]
    best = jnp.full((1, slots), -1.0, jnp.float32)
    jobs = [(0, 4, 0, every), (0, 4, 1, every), (0, 4, 2, (0, 2)), (0, 4, 3, (0, 2))]
    some = given((0, 2), range(4)) | given((1, 3), range(2))
    (best,) = compare(cap, row, jobs, some, best)
    across[3], best = tie(across[3], best)
    beyond[3] = core(across[3])
    some = given((0,), range(4)) | given((1, 3), (2,))
    (best,) = compare(cap, row, [(0, 4, 2, (1, 3))], some, best)
    some = given((0,), range(4)) | given((1, 3), (3,))
    best = compare(cap, pieces, [(0, 4, 3, (1, 3))], some, best)
    backs = [exchange(b, low, 1, -1) for b, (low, _) in zip(best, pieces)]
    return unpack(slot, backs).reshape(rows)


def solution(mesh):
    placed = (P(("parts", "blk"), None), P(("parts", "blk")), P(("parts", "blk")))
    return jax.shard_map(
        on_device, mesh=mesh, in_specs=placed, out_specs=P(("parts", "blk")), check_vma=False
    )
```

```python
import jax
import jax.numpy as jnp
from jax import lax
from jax.experimental import pallas as pl
from jax.experimental.pallas import tpu as pltpu
from jax.sharding import PartitionSpec as P

GROUP = 4
BLOCKS = 4
UNITS = (4, 4, 4, 4)
PAD = 16
STEP = 512
GRANT = 16 << 20
NT = (((1,), (1,)), ((), ()))


def iota(shape, axis):
    return lax.broadcasted_iota(jnp.int32, shape, axis)


def spans(widths):
    start, out = 0, []
    for width in widths:
        out.append((start, width))
        start += width
    return out


def pack_kernel(groups, cap, units, emb_hbm, owner_hbm, cluster_hbm, *refs):
    blocks, refs = refs[: len(units)], refs[len(units) :]
    slot_ref, emb_ref, unit_ref, owner_ref, cluster_ref, sems = refs
    rows = emb_ref.shape[0]
    part = rows // 4
    copies = [
        pltpu.make_async_copy(owner_hbm, owner_ref, sems.at[0]),
        pltpu.make_async_copy(cluster_hbm, cluster_ref, sems.at[1]),
    ]
    for i in range(4):
        span = pl.ds(i * part, part)
        copies.append(pltpu.make_async_copy(emb_hbm.at[span], emb_ref.at[span], sems.at[2 + i]))
    for copy in copies:
        copy.start()
    earlier = (iota((rows, rows), 0) < iota((rows, rows), 1)).astype(jnp.bfloat16)
    mine = lax.axis_index("blk") // GROUP
    copies[0].wait()
    rel = ((owner_ref[...] >> 2) - mine + groups) & (groups - 1)
    place = jnp.where(rel > groups // 2, 2 * (groups - rel), jnp.maximum(2 * rel - 1, 0))
    member = iota((max(groups, 16), rows), 0) == place
    count = jnp.dot(member.astype(jnp.bfloat16), earlier, preferred_element_type=jnp.float32)
    rank = jnp.sum(jnp.where(member, count, 0.0), axis=0, keepdims=True)
    slot = place * cap + rank.astype(jnp.int32)
    slot_ref[...] = slot
    copies[1].wait()
    label = ((cluster_ref[...] & 15) + 1).astype(jnp.float32).astype(jnp.bfloat16)
    label = jnp.broadcast_to(label, (PAD, rows))
    for i in range(4):
        copies[2 + i].wait()
        x = emb_ref[i * part : (i + 1) * part, :]
        squares = jnp.sum(x * x, axis=1, keepdims=True)
        unit_ref[i * part : (i + 1) * part, :] = (x * lax.rsqrt(squares + 1e-06)).astype(
            jnp.bfloat16
        )
    unit = unit_ref[...]
    for ref, (start, size) in zip(blocks, units):
        hot = (iota((size, rows), 0) + start == slot).astype(jnp.bfloat16)
        packed = jnp.dot(hot, unit, preferred_element_type=jnp.float32).astype(jnp.bfloat16)
        marks = lax.dot_general(label, hot, NT, preferred_element_type=jnp.float32)
        marks = (marks - 1.0).astype(jnp.bfloat16)
        sub = min(cap, size)
        for i in range(size // sub):
            low = i * (sub + PAD)
            ref[low : low + sub, :] = packed[i * sub : (i + 1) * sub, :]
            ref[low + sub : low + sub + PAD, :] = jnp.zeros((PAD, unit.shape[1]), jnp.bfloat16)
            ref[low + sub : low + sub + PAD, 0:sub] = marks[:, i * sub : (i + 1) * sub]


def pack(groups, cap, units, embedding, owner, cluster):
    rows, width = embedding.shape
    return pl.pallas_call(
        lambda *refs: pack_kernel(groups, cap, units, *refs),
        in_specs=[pl.BlockSpec(memory_space=pltpu.HBM)] * 3,
        out_shape=[
            jax.ShapeDtypeStruct((n + n // min(cap, n) * PAD, width), jnp.bfloat16)
            for _, n in units
        ]
        + [jax.ShapeDtypeStruct((1, rows), jnp.int32)],
        scratch_shapes=[
            pltpu.VMEM((rows, width), jnp.float32),
            pltpu.VMEM((rows, width), jnp.bfloat16),
            pltpu.VMEM((1, rows), jnp.int32),
            pltpu.VMEM((1, rows), jnp.int32),
            pltpu.SemaphoreType.DMA((6,)),
        ],
        name="pack",
    )(embedding, owner.reshape(1, rows), cluster.reshape(1, rows))


def compare_kernel(cap, outs, jobs, names, *refs):
    best_ref, refs = refs[0], refs[1:]
    given = {}
    for name, ref in zip(names, refs):
        given.setdefault(name, []).append(ref)
    refs = refs[len(names) :]
    outputs, scratch = refs[: len(outs)], list(refs[len(outs) :])
    query_ref = scratch.pop()
    size = query_ref.shape[0] // BLOCKS

    def unfold(parts, target, low):
        for ref in parts:
            sub = min(cap, size // len(parts))
            for start in range(0, ref.shape[0], sub + PAD):
                target[low : low + sub, :] = ref[start : start + sub, :]
                low += sub

    keys, marks = {}, {}
    for (peer, k), parts in given.items():
        sub = min(cap, size // len(parts))
        row = [
            ref[start + sub : start + sub + PAD, 0:sub].astype(jnp.float32)
            for ref in parts
            for start in range(0, ref.shape[0], sub + PAD)
        ]
        marks[peer, k] = jnp.concatenate(row, axis=1)[0:1, :]
        if peer == 0:
            unfold(parts, query_ref, k * size)
            keys[peer, k] = query_ref.at[k * size : (k + 1) * size]
        elif size == sub:
            keys[peer, k] = parts[0].at[0:size]
        else:
            keys[peer, k] = scratch.pop()
            unfold(parts, keys[peer, k], 0)
    columns = {}
    for k in range(BLOCKS):
        table = [marks.get((peer, k), marks[0, k]) for peer in range(4)]
        columns[k] = jnp.concatenate(table * 2, axis=0).T
    near = jnp.concatenate([marks[0, k] for k in range(BLOCKS)], axis=1)
    bests = [best_ref[:, k * size : (k + 1) * size] for k in range(BLOCKS)]
    for low, high, k, peers in jobs:
        for left in range(low, high, STEP // size):
            right = min(left + STEP // size, high)
            span = slice(left * size, right * size)
            row = near[0:1, span]
            best = None
            for peer in peers:
                scores = lax.dot_general(
                    keys[peer, k][...],
                    query_ref[span, :],
                    NT,
                    preferred_element_type=jnp.float32,
                )
                allowed = columns[k][:, peer : peer + 1] == row
                if peer == 0 and left <= k < right:
                    shift = (k - left) * size
                    allowed = allowed & (iota(scores.shape, 0) + shift != iota(scores.shape, 1))
                top = jnp.max(jnp.where(allowed, scores, -1.0), axis=0, keepdims=True)
                best = top if best is None else jnp.maximum(best, top)
            for q in range(left, right):
                part = best[:, (q - left) * size : (q - left + 1) * size]
                bests[q] = jnp.maximum(bests[q], part)
    for q in range(BLOCKS):
        spread(outputs, outs, q * size, bests[q])


def spread(refs, outs, start, row):
    for ref, (low, width) in zip(refs, outs):
        a, b = max(low, start), min(low + width, start + row.shape[1])
        if a < b:
            ref[:, a - low : b - low] = row[:, a - start : b - start]


def compare(cap, outs, jobs, blocks, best):
    slots, width = best.shape[1], blocks[0, 0][0].shape[1]
    size = slots // BLOCKS
    tiles = sum((high - low) * len(peers) for low, high, _, peers in jobs)
    folded = [key for key, parts in blocks.items() if key[0] and size > min(cap, size // len(parts))]
    names = tuple(key for key, parts in blocks.items() for _ in parts)
    return pl.pallas_call(
        lambda *refs: compare_kernel(cap, outs, jobs, names, *refs),
        out_shape=[jax.ShapeDtypeStruct((1, n), jnp.float32) for _, n in outs],
        scratch_shapes=[pltpu.VMEM((size, width), jnp.bfloat16)] * len(folded)
        + [pltpu.VMEM((slots, width), jnp.bfloat16)],
        compiler_params=pltpu.CompilerParams(vmem_limit_bytes=GRANT),
        cost_estimate=pl.CostEstimate(
            flops=2 * tiles * size * size * width, bytes_accessed=0, transcendentals=0
        ),
        name=f"compare{len(jobs)}_{tiles}",
    )(best, *[part for parts in blocks.values() for part in parts])


def unpack_kernel(slot_ref, *refs):
    out_ref = refs[-1]
    slot = slot_ref[...]
    rows = slot.shape[1]
    total = jnp.zeros((8, rows), jnp.float32)
    start = 0
    for ref in refs[:-1]:
        size = ref.shape[1]
        column = jnp.broadcast_to(ref[...], (8, size)).T[:, 0:1]
        hit = iota((size, rows), 0) + start == slot
        part = jnp.where(hit, column, 0.0)
        total = total + jnp.sum(part.reshape(size // 8, 8, rows), axis=0)
        start += size
    out_ref[...] = jnp.sum(total, axis=0, keepdims=True)


def unpack(slot, backs):
    return pl.pallas_call(
        unpack_kernel,
        out_shape=jax.ShapeDtypeStruct(slot.shape, jnp.float32),
        compiler_params=pltpu.CompilerParams(vmem_limit_bytes=GRANT),
        name="unpack",
    )(slot, *backs)


def join(parts, axis):
    return parts[0] if len(parts) == 1 else jnp.concatenate(parts, axis=axis)


def on_device(embedding, row_owner, cluster_id):
    rows, _ = embedding.shape
    devices = lax.axis_size("blk")
    groups = devices // GROUP
    cap = GROUP * max(2, 2 * rows // devices)
    slots = groups * cap
    units = spans([slots // 16 * n for n in UNITS])
    pieces = spans([max(cap, 128)] * (slots // max(cap, 128)))
    shifts = [0] + [(k + 1) // 2 if k % 2 else groups - k // 2 for k in range(1, groups)]

    def shift(array, distance):
        step = distance * GROUP
        return lax.ppermute(array, "blk", [(i, (i + step) % devices) for i in range(devices)])

    def swap(array, mask):
        return lax.ppermute(array, "blk", [(i, i ^ mask) for i in range(devices)])

    def exchange(array, start, axis, sign):
        size, out = array.shape[axis], []
        for k in range(start // cap, (start + size - 1) // cap + 1):
            a, b = max(k * cap - start, 0), min((k + 1) * cap - start, size)
            part = lax.slice_in_dim(array, a, b, axis=axis)
            out.append(shift(part, sign * shifts[k]) if shifts[k] else part)
        return join(out, axis)

    *blocks, slot = pack(groups, cap, units, embedding, row_owner, cluster_id)

    def tie(*arrays):
        return lax.optimization_barrier(arrays)

    def send(u):
        (start, size), out = units[u], []
        sub = min(cap, size)
        for i in range(size // sub):
            part = lax.slice_in_dim(blocks[u], i * (sub + PAD), (i + 1) * (sub + PAD))
            distance = shifts[(start + i * sub) // cap]
            out.append(shift(part, distance) if distance else part)
        return join(out, 0)

    def cross(parts):
        return [swap(part, 2) for part in parts]

    def core(parts):
        return [swap(part, 1) for part in parts]

    arrays = [[None] * BLOCKS for _ in range(4)]
    own, across, beside, beyond = arrays
    sent = [blocks[0]] + [send(u) for u in range(1, len(units))]
    own[:] = [sent[0]], [sent[1]], [sent[2]], sent[3:]
    for u in range(BLOCKS):
        beside[u], across[u] = core(own[u]), cross(own[u])
    for u in range(BLOCKS - 1):
        beyond[u] = core(across[u])

    def given(peers, blocks):
        return {(peer, k): arrays[peer][k] for peer in peers for k in blocks}

    every, row = (0, 1, 2, 3), [(0, slots)]
    best = jnp.full((1, slots), -1.0, jnp.float32)
    jobs = [(0, 4, 0, every), (0, 4, 1, every), (0, 4, 2, every), (0, 4, 3, (0, 2))]
    some = given((0, 2), range(4)) | given((1, 3), range(3))
    (best,) = compare(cap, row, jobs, some, best)
    across[3][-1], best = tie(across[3][-1], best)
    beyond[3] = core(across[3])
    some = given((0,), range(4)) | given((1, 3), (3,))
    best = compare(cap, pieces, [(0, 4, 3, (1, 3))], some, best)
    backs = [exchange(b, low, 1, -1) for b, (low, _) in zip(best, pieces)]
    return unpack(slot, backs).reshape(rows)


def solution(mesh):
    placed = (P(("parts", "blk"), None), P(("parts", "blk")), P(("parts", "blk")))
    return jax.shard_map(
        on_device, mesh=mesh, in_specs=placed, out_specs=P(("parts", "blk")), check_vma=False
    )
```

```python
import jax
import jax.numpy as jnp
from jax import lax
from jax.experimental import pallas as pl
from jax.experimental.pallas import tpu as pltpu
from jax.sharding import PartitionSpec as P

GROUP = 4
BLOCKS = 4
UNITS = (4, 4, 4, 4)
PAD = 16
STEP = 512
GRANT = 16 << 20
NT = (((1,), (1,)), ((), ()))


def iota(shape, axis):
    return lax.broadcasted_iota(jnp.int32, shape, axis)


def spans(widths):
    start, out = 0, []
    for width in widths:
        out.append((start, width))
        start += width
    return out


def pack_kernel(groups, cap, units, emb_hbm, owner_hbm, cluster_hbm, *refs):
    blocks, refs = refs[: len(units)], refs[len(units) :]
    slot_ref, emb_ref, unit_ref, owner_ref, cluster_ref, sems = refs
    rows = emb_ref.shape[0]
    part = rows // 4
    copies = [
        pltpu.make_async_copy(owner_hbm, owner_ref, sems.at[0]),
        pltpu.make_async_copy(cluster_hbm, cluster_ref, sems.at[1]),
    ]
    for i in range(4):
        span = pl.ds(i * part, part)
        copies.append(pltpu.make_async_copy(emb_hbm.at[span], emb_ref.at[span], sems.at[2 + i]))
    for copy in copies:
        copy.start()
    earlier = (iota((rows, rows), 0) < iota((rows, rows), 1)).astype(jnp.bfloat16)
    mine = lax.axis_index("blk") // GROUP
    copies[0].wait()
    rel = ((owner_ref[...] >> 2) - mine + groups) & (groups - 1)
    place = jnp.where(rel > groups // 2, 2 * (groups - rel), jnp.maximum(2 * rel - 1, 0))
    member = iota((max(groups, 16), rows), 0) == place
    count = jnp.dot(member.astype(jnp.bfloat16), earlier, preferred_element_type=jnp.float32)
    rank = jnp.sum(jnp.where(member, count, 0.0), axis=0, keepdims=True)
    slot = place * cap + rank.astype(jnp.int32)
    slot_ref[...] = (owner_ref[...] >> 2) * cap + rank.astype(jnp.int32)
    copies[1].wait()
    label = ((cluster_ref[...] & 15) + 1).astype(jnp.float32).astype(jnp.bfloat16)
    label = jnp.broadcast_to(label, (PAD, rows))
    for i in range(4):
        copies[2 + i].wait()
        x = emb_ref[i * part : (i + 1) * part, :]
        squares = jnp.sum(x * x, axis=1, keepdims=True)
        unit_ref[i * part : (i + 1) * part, :] = (x * lax.rsqrt(squares + 1e-06)).astype(
            jnp.bfloat16
        )
    unit = unit_ref[...]
    for ref, (start, size) in zip(blocks, units):
        hot = (iota((size, rows), 0) + start == slot).astype(jnp.bfloat16)
        packed = jnp.dot(hot, unit, preferred_element_type=jnp.float32).astype(jnp.bfloat16)
        marks = lax.dot_general(label, hot, NT, preferred_element_type=jnp.float32)
        marks = (marks - 1.0).astype(jnp.bfloat16)
        sub = min(cap, size)
        for i in range(size // sub):
            low = i * (sub + PAD)
            ref[low : low + sub, :] = packed[i * sub : (i + 1) * sub, :]
            ref[low + sub : low + sub + PAD, :] = jnp.zeros((PAD, unit.shape[1]), jnp.bfloat16)
            ref[low + sub : low + sub + PAD, 0:sub] = marks[:, i * sub : (i + 1) * sub]


def pack(groups, cap, units, embedding, owner, cluster):
    rows, width = embedding.shape
    return pl.pallas_call(
        lambda *refs: pack_kernel(groups, cap, units, *refs),
        in_specs=[pl.BlockSpec(memory_space=pltpu.HBM)] * 3,
        out_shape=[
            jax.ShapeDtypeStruct((n + n // min(cap, n) * PAD, width), jnp.bfloat16)
            for _, n in units
        ]
        + [jax.ShapeDtypeStruct((1, rows), jnp.int32)],
        scratch_shapes=[
            pltpu.VMEM((rows, width), jnp.float32),
            pltpu.VMEM((rows, width), jnp.bfloat16),
            pltpu.VMEM((1, rows), jnp.int32),
            pltpu.VMEM((1, rows), jnp.int32),
            pltpu.SemaphoreType.DMA((6,)),
        ],
        name="pack",
    )(embedding, owner.reshape(1, rows), cluster.reshape(1, rows))


def compare_kernel(cap, outs, jobs, names, *refs):
    best_ref, refs = refs[0], refs[1:]
    given = {}
    for name, ref in zip(names, refs):
        given.setdefault(name, []).append(ref)
    refs = refs[len(names) :]
    outputs, scratch = refs[: max(len(outs), 1)], list(refs[max(len(outs), 1) :])
    query_ref = scratch.pop()
    size = query_ref.shape[0] // BLOCKS

    def unfold(parts, target, low):
        for ref in parts:
            sub = min(cap, size // len(parts))
            for start in range(0, ref.shape[0], sub + PAD):
                target[low : low + sub, :] = ref[start : start + sub, :]
                low += sub

    keys, marks = {}, {}
    for (peer, k), parts in given.items():
        sub = min(cap, size // len(parts))
        row = [
            ref[start + sub : start + sub + PAD, 0:sub].astype(jnp.float32)
            for ref in parts
            for start in range(0, ref.shape[0], sub + PAD)
        ]
        marks[peer, k] = jnp.concatenate(row, axis=1)[0:1, :]
        if peer == 0:
            unfold(parts, query_ref, k * size)
            keys[peer, k] = query_ref.at[k * size : (k + 1) * size]
        elif size == sub:
            keys[peer, k] = parts[0].at[0:size]
        else:
            keys[peer, k] = scratch.pop()
            unfold(parts, keys[peer, k], 0)
    columns = {}
    for k in range(BLOCKS):
        table = [marks.get((peer, k), marks[0, k]) for peer in range(4)]
        columns[k] = jnp.concatenate(table * 2, axis=0).T
    near = jnp.concatenate([marks[0, k] for k in range(BLOCKS)], axis=1)
    bests = [best_ref[:, k * size : (k + 1) * size] for k in range(BLOCKS)]
    for low, high, k, peers in jobs:
        for left in range(low, high, STEP // size):
            right = min(left + STEP // size, high)
            span = slice(left * size, right * size)
            row = near[0:1, span]
            best = None
            for peer in peers:
                scores = lax.dot_general(
                    keys[peer, k][...],
                    query_ref[span, :],
                    NT,
                    preferred_element_type=jnp.float32,
                )
                allowed = columns[k][:, peer : peer + 1] == row
                if peer == 0 and left <= k < right:
                    shift = (k - left) * size
                    allowed = allowed & (iota(scores.shape, 0) + shift != iota(scores.shape, 1))
                top = jnp.max(jnp.where(allowed, scores, -1.0), axis=0, keepdims=True)
                best = top if best is None else jnp.maximum(best, top)
            for q in range(left, right):
                part = best[:, (q - left) * size : (q - left + 1) * size]
                bests[q] = jnp.maximum(bests[q], part)
    if not outs:
        whole = jnp.concatenate(bests, axis=1)
        groups = whole.shape[1] // cap
        mine = lax.axis_index("blk") // GROUP
        for k in range(groups):
            step = (k + 1) // 2 if k % 2 else groups - k // 2
            source = (mine - step + groups) & (groups - 1)
            outputs[0][pl.ds(source, 1), :] = whole[:, k * cap : (k + 1) * cap]
    for q in range(BLOCKS if outs else 0):
        spread(outputs, outs, q * size, bests[q])


def spread(refs, outs, start, row):
    for ref, (low, width) in zip(refs, outs):
        a, b = max(low, start), min(low + width, start + row.shape[1])
        if a < b:
            ref[:, a - low : b - low] = row[:, a - start : b - start]


def compare(cap, outs, jobs, blocks, best):
    slots, width = best.shape[1], blocks[0, 0][0].shape[1]
    size = slots // BLOCKS
    tiles = sum((high - low) * len(peers) for low, high, _, peers in jobs)
    folded = [key for key, parts in blocks.items() if key[0] and size > min(cap, size // len(parts))]
    names = tuple(key for key, parts in blocks.items() for _ in parts)
    return pl.pallas_call(
        lambda *refs: compare_kernel(cap, outs, jobs, names, *refs),
        out_shape=[
            jax.ShapeDtypeStruct(shape, jnp.float32)
            for shape in [(1, n) for _, n in outs] or [(slots // cap, cap)]
        ],
        scratch_shapes=[pltpu.VMEM((size, width), jnp.bfloat16)] * len(folded)
        + [pltpu.VMEM((slots, width), jnp.bfloat16)],
        compiler_params=pltpu.CompilerParams(vmem_limit_bytes=GRANT),
        cost_estimate=pl.CostEstimate(
            flops=2 * tiles * size * size * width, bytes_accessed=0, transcendentals=0
        ),
        name=f"compare{len(jobs)}_{tiles}",
    )(best, *[part for parts in blocks.values() for part in parts])


def unpack_kernel(slot_ref, back_ref, out_ref):
    slot = slot_ref[...]
    rows = slot.shape[1]
    count, size = back_ref.shape
    table = jnp.concatenate([back_ref[...]] * max(8 // count, 1), axis=0).T
    total = jnp.zeros((8, rows), jnp.float32)
    for i in range(count):
        hit = iota((size, rows), 0) + i * size == slot
        part = jnp.where(hit, table[:, i : i + 1], 0.0)
        total = total + jnp.sum(part.reshape(size // 8, 8, rows), axis=0)
    out_ref[...] = jnp.sum(total, axis=0, keepdims=True)


def unpack(slot, back):
    return pl.pallas_call(
        unpack_kernel,
        out_shape=jax.ShapeDtypeStruct(slot.shape, jnp.float32),
        compiler_params=pltpu.CompilerParams(vmem_limit_bytes=GRANT),
        name="unpack",
    )(slot, back)


def join(parts, axis):
    return parts[0] if len(parts) == 1 else jnp.concatenate(parts, axis=axis)


def on_device(embedding, row_owner, cluster_id):
    rows, _ = embedding.shape
    devices = lax.axis_size("blk")
    groups = devices // GROUP
    cap = GROUP * max(2, 2 * rows // devices)
    slots = groups * cap
    units = spans([slots // 16 * n for n in UNITS])
    shifts = [0] + [(k + 1) // 2 if k % 2 else groups - k // 2 for k in range(1, groups)]

    def shift(array, distance):
        step = distance * GROUP
        return lax.ppermute(array, "blk", [(i, (i + step) % devices) for i in range(devices)])

    def swap(array, mask):
        return lax.ppermute(array, "blk", [(i, i ^ mask) for i in range(devices)])

    *blocks, slot = pack(groups, cap, units, embedding, row_owner, cluster_id)

    def tie(*arrays):
        return lax.optimization_barrier(arrays)

    def send(u):
        (start, size), out = units[u], []
        sub = min(cap, size)
        for i in range(size // sub):
            part = lax.slice_in_dim(blocks[u], i * (sub + PAD), (i + 1) * (sub + PAD))
            distance = shifts[(start + i * sub) // cap]
            out.append(shift(part, distance) if distance else part)
        return join(out, 0)

    def cross(parts):
        return [swap(part, 2) for part in parts]

    def core(parts):
        return [swap(part, 1) for part in parts]

    arrays = [[None] * BLOCKS for _ in range(4)]
    own, across, beside, beyond = arrays
    sent = [blocks[0], send(1)]
    blocks[2], blocks[3], sent[1] = tie(blocks[2], blocks[3], sent[1])
    sent += [send(2), send(3)]
    own[:] = [sent[0]], [sent[1]], [sent[2]], sent[3:]
    for u in range(BLOCKS):
        beside[u], across[u] = core(own[u]), cross(own[u])
    for u in range(BLOCKS - 1):
        beyond[u] = core(across[u])

    def given(peers, blocks):
        return {(peer, k): arrays[peer][k] for peer in peers for k in blocks}

    every, row = (0, 1, 2, 3), [(0, slots)]
    best = jnp.full((1, slots), -1.0, jnp.float32)
    jobs = [(0, 4, 0, every), (0, 4, 1, every), (0, 4, 2, (0, 2)), (0, 4, 3, (0, 2))]
    some = given((0, 2), range(4)) | given((1, 3), range(2))
    (best,) = compare(cap, row, jobs, some, best)
    across[3][-1], best = tie(across[3][-1], best)
    beyond[3] = core(across[3])
    some = given((0,), range(4)) | given((1, 3), (2,))
    (best,) = compare(cap, row, [(0, 4, 2, (1, 3))], some, best)
    some = given((0,), range(4)) | given((1, 3), (3,))
    (best,) = compare(cap, [], [(0, 4, 3, (1, 3))], some, best)
    rings = [[g * GROUP + p for g in range(groups)] for p in range(GROUP)]
    back = lax.all_to_all(
        best, "blk", split_axis=0, concat_axis=0, tiled=True, axis_index_groups=rings
    )
    wide = max(cap, 128)
    return unpack(slot, back.reshape(slots // wide, wide)).reshape(rows)


def solution(mesh):
    placed = (P(("parts", "blk"), None), P(("parts", "blk")), P(("parts", "blk")))
    return jax.shard_map(
        on_device, mesh=mesh, in_specs=placed, out_specs=P(("parts", "blk")), check_vma=False
    )
```

```python
import jax
import jax.numpy as jnp
from jax import lax
from jax.experimental import pallas as pl
from jax.experimental.pallas import tpu as pltpu
from jax.sharding import PartitionSpec as P

GROUP = 4
BLOCKS = 4
UNITS = (4, 4, 4, 2, 2)
PAD = 16
STEP = 512
GRANT = 16 << 20
NT = (((1,), (1,)), ((), ()))


def iota(shape, axis):
    return lax.broadcasted_iota(jnp.int32, shape, axis)


def spans(widths):
    start, out = 0, []
    for width in widths:
        out.append((start, width))
        start += width
    return out


def pack_kernel(groups, cap, units, emb_hbm, owner_hbm, cluster_hbm, *refs):
    blocks, refs = refs[: len(units)], refs[len(units) :]
    slot_ref, emb_ref, unit_ref, owner_ref, cluster_ref, sems = refs
    rows = emb_ref.shape[0]
    part = rows // 4
    copies = [
        pltpu.make_async_copy(owner_hbm, owner_ref, sems.at[0]),
        pltpu.make_async_copy(cluster_hbm, cluster_ref, sems.at[1]),
    ]
    for i in range(4):
        span = pl.ds(i * part, part)
        copies.append(pltpu.make_async_copy(emb_hbm.at[span], emb_ref.at[span], sems.at[2 + i]))
    for copy in copies:
        copy.start()
    earlier = (iota((rows, rows), 0) < iota((rows, rows), 1)).astype(jnp.bfloat16)
    mine = lax.axis_index("blk") // GROUP
    copies[0].wait()
    rel = ((owner_ref[...] >> 2) - mine + groups) & (groups - 1)
    place = jnp.where(rel > groups // 2, 2 * (groups - rel), jnp.maximum(2 * rel - 1, 0))
    member = iota((max(groups, 16), rows), 0) == place
    count = jnp.dot(member.astype(jnp.bfloat16), earlier, preferred_element_type=jnp.float32)
    rank = jnp.sum(jnp.where(member, count, 0.0), axis=0, keepdims=True)
    slot = place * cap + rank.astype(jnp.int32)
    slot_ref[...] = slot
    copies[1].wait()
    label = ((cluster_ref[...] & 15) + 1).astype(jnp.float32).astype(jnp.bfloat16)
    label = jnp.broadcast_to(label, (PAD, rows))
    for i in range(4):
        copies[2 + i].wait()
        x = emb_ref[i * part : (i + 1) * part, :]
        squares = jnp.sum(x * x, axis=1, keepdims=True)
        unit_ref[i * part : (i + 1) * part, :] = (x * lax.rsqrt(squares + 1e-06)).astype(
            jnp.bfloat16
        )
    unit = unit_ref[...]
    for ref, (start, size) in zip(blocks, units):
        hot = (iota((size, rows), 0) + start == slot).astype(jnp.bfloat16)
        packed = jnp.dot(hot, unit, preferred_element_type=jnp.float32).astype(jnp.bfloat16)
        marks = lax.dot_general(label, hot, NT, preferred_element_type=jnp.float32)
        marks = (marks - 1.0).astype(jnp.bfloat16)
        sub = min(cap, size)
        for i in range(size // sub):
            low = i * (sub + PAD)
            ref[low : low + sub, :] = packed[i * sub : (i + 1) * sub, :]
            ref[low + sub : low + sub + PAD, :] = jnp.zeros((PAD, unit.shape[1]), jnp.bfloat16)
            ref[low + sub : low + sub + PAD, 0:sub] = marks[:, i * sub : (i + 1) * sub]


def pack(groups, cap, units, embedding, owner, cluster):
    rows, width = embedding.shape
    return pl.pallas_call(
        lambda *refs: pack_kernel(groups, cap, units, *refs),
        in_specs=[pl.BlockSpec(memory_space=pltpu.HBM)] * 3,
        out_shape=[
            jax.ShapeDtypeStruct((n + n // min(cap, n) * PAD, width), jnp.bfloat16)
            for _, n in units
        ]
        + [jax.ShapeDtypeStruct((1, rows), jnp.int32)],
        scratch_shapes=[
            pltpu.VMEM((rows, width), jnp.float32),
            pltpu.VMEM((rows, width), jnp.bfloat16),
            pltpu.VMEM((1, rows), jnp.int32),
            pltpu.VMEM((1, rows), jnp.int32),
            pltpu.SemaphoreType.DMA((6,)),
        ],
        name="pack",
    )(embedding, owner.reshape(1, rows), cluster.reshape(1, rows))


def compare_kernel(cap, outs, jobs, names, *refs):
    best_ref, refs = refs[0], refs[1:]
    given = {}
    for name, ref in zip(names, refs):
        given.setdefault(name, []).append(ref)
    refs = refs[len(names) :]
    outputs, scratch = refs[: len(outs)], list(refs[len(outs) :])
    query_ref = scratch.pop()
    size = query_ref.shape[0] // BLOCKS

    def unfold(parts, target, low):
        for ref in parts:
            sub = min(cap, size // len(parts))
            for start in range(0, ref.shape[0], sub + PAD):
                target[low : low + sub, :] = ref[start : start + sub, :]
                low += sub

    keys, marks = {}, {}
    for (peer, k), parts in given.items():
        sub = min(cap, size // len(parts))
        row = [
            ref[start + sub : start + sub + PAD, 0:sub].astype(jnp.float32)
            for ref in parts
            for start in range(0, ref.shape[0], sub + PAD)
        ]
        marks[peer, k] = jnp.concatenate(row, axis=1)[0:1, :]
        if peer == 0:
            unfold(parts, query_ref, k * size)
            keys[peer, k] = query_ref.at[k * size : (k + 1) * size]
        elif size == sub:
            keys[peer, k] = parts[0].at[0:size]
        else:
            keys[peer, k] = scratch.pop()
            unfold(parts, keys[peer, k], 0)
    columns = {}
    for k in range(BLOCKS):
        table = [marks.get((peer, k), marks[0, k]) for peer in range(4)]
        columns[k] = jnp.concatenate(table * 2, axis=0).T
    near = jnp.concatenate([marks[0, k] for k in range(BLOCKS)], axis=1)
    bests = [best_ref[:, k * size : (k + 1) * size] for k in range(BLOCKS)]
    for low, high, k, peers in jobs:
        for left in range(low, high, STEP // size):
            right = min(left + STEP // size, high)
            span = slice(left * size, right * size)
            row = near[0:1, span]
            best = None
            for peer in peers:
                scores = lax.dot_general(
                    keys[peer, k][...],
                    query_ref[span, :],
                    NT,
                    preferred_element_type=jnp.float32,
                )
                allowed = columns[k][:, peer : peer + 1] == row
                if peer == 0 and left <= k < right:
                    shift = (k - left) * size
                    allowed = allowed & (iota(scores.shape, 0) + shift != iota(scores.shape, 1))
                top = jnp.max(jnp.where(allowed, scores, -1.0), axis=0, keepdims=True)
                best = top if best is None else jnp.maximum(best, top)
            for q in range(left, right):
                part = best[:, (q - left) * size : (q - left + 1) * size]
                bests[q] = jnp.maximum(bests[q], part)
    for q in range(BLOCKS):
        spread(outputs, outs, q * size, bests[q])


def spread(refs, outs, start, row):
    for ref, (low, width) in zip(refs, outs):
        a, b = max(low, start), min(low + width, start + row.shape[1])
        if a < b:
            ref[:, a - low : b - low] = row[:, a - start : b - start]


def compare(cap, outs, jobs, blocks, best):
    slots, width = best.shape[1], blocks[0, 0][0].shape[1]
    size = slots // BLOCKS
    tiles = sum((high - low) * len(peers) for low, high, _, peers in jobs)
    folded = [key for key, parts in blocks.items() if key[0] and size > min(cap, size // len(parts))]
    names = tuple(key for key, parts in blocks.items() for _ in parts)
    return pl.pallas_call(
        lambda *refs: compare_kernel(cap, outs, jobs, names, *refs),
        out_shape=[jax.ShapeDtypeStruct((1, n), jnp.float32) for _, n in outs],
        scratch_shapes=[pltpu.VMEM((size, width), jnp.bfloat16)] * len(folded)
        + [pltpu.VMEM((slots, width), jnp.bfloat16)],
        compiler_params=pltpu.CompilerParams(vmem_limit_bytes=GRANT),
        cost_estimate=pl.CostEstimate(
            flops=2 * tiles * size * size * width, bytes_accessed=0, transcendentals=0
        ),
        name=f"compare{len(jobs)}_{tiles}",
    )(best, *[part for parts in blocks.values() for part in parts])


def unpack_kernel(slot_ref, *refs):
    out_ref = refs[-1]
    slot = slot_ref[...]
    rows = slot.shape[1]
    total = jnp.zeros((8, rows), jnp.float32)
    start = 0
    for ref in refs[:-1]:
        size = ref.shape[1]
        column = jnp.broadcast_to(ref[...], (8, size)).T[:, 0:1]
        hit = iota((size, rows), 0) + start == slot
        part = jnp.where(hit, column, 0.0)
        total = total + jnp.sum(part.reshape(size // 8, 8, rows), axis=0)
        start += size
    out_ref[...] = jnp.sum(total, axis=0, keepdims=True)


def unpack(slot, backs):
    return pl.pallas_call(
        unpack_kernel,
        out_shape=jax.ShapeDtypeStruct(slot.shape, jnp.float32),
        compiler_params=pltpu.CompilerParams(vmem_limit_bytes=GRANT),
        name="unpack",
    )(slot, *backs)


def join(parts, axis):
    return parts[0] if len(parts) == 1 else jnp.concatenate(parts, axis=axis)


def on_device(embedding, row_owner, cluster_id):
    rows, _ = embedding.shape
    devices = lax.axis_size("blk")
    groups = devices // GROUP
    cap = GROUP * max(2, 2 * rows // devices)
    slots = groups * cap
    units = spans([slots // 16 * n for n in UNITS])
    pieces = spans([max(cap, 128)] * (slots // max(cap, 128)))
    shifts = [0] + [(k + 1) // 2 if k % 2 else groups - k // 2 for k in range(1, groups)]

    def shift(array, distance):
        step = distance * GROUP
        return lax.ppermute(array, "blk", [(i, (i + step) % devices) for i in range(devices)])

    def swap(array, mask):
        return lax.ppermute(array, "blk", [(i, i ^ mask) for i in range(devices)])

    def exchange(array, start, axis, sign):
        size, out = array.shape[axis], []
        for k in range(start // cap, (start + size - 1) // cap + 1):
            a, b = max(k * cap - start, 0), min((k + 1) * cap - start, size)
            part = lax.slice_in_dim(array, a, b, axis=axis)
            out.append(shift(part, sign * shifts[k]) if shifts[k] else part)
        return join(out, axis)

    *blocks, slot = pack(groups, cap, units, embedding, row_owner, cluster_id)

    def tie(*arrays):
        return lax.optimization_barrier(arrays)

    def send(u):
        (start, size), out = units[u], []
        sub = min(cap, size)
        for i in range(size // sub):
            part = lax.slice_in_dim(blocks[u], i * (sub + PAD), (i + 1) * (sub + PAD))
            distance = shifts[(start + i * sub) // cap]
            out.append(shift(part, distance) if distance else part)
        return join(out, 0)

    def cross(parts):
        return [swap(part, 2) for part in parts]

    def core(parts):
        return [swap(part, 1) for part in parts]

    arrays = [[None] * BLOCKS for _ in range(4)]
    own, across, beside, beyond = arrays
    sent = [blocks[0], send(1)]
    blocks[2], blocks[3], sent[1] = tie(blocks[2], blocks[3], sent[1])
    sent += [send(2), send(3)]
    blocks[4], sent[2] = tie(blocks[4], sent[2])
    sent += [send(4)]
    own[:] = [sent[0]], [sent[1]], [sent[2]], sent[3:]
    across[0] = cross(own[0])
    own[0][0], own[2][0] = tie(own[0][0], own[2][0])
    beside[0] = core(own[0])
    for u in range(1, BLOCKS):
        beside[u], across[u] = core(own[u]), cross(own[u])
    for u in range(BLOCKS - 1):
        beyond[u] = core(across[u])

    def given(peers, blocks):
        return {(peer, k): arrays[peer][k] for peer in peers for k in blocks}

    every, row = (0, 1, 2, 3), [(0, slots)]
    best = jnp.full((1, slots), -1.0, jnp.float32)
    best, across[3][0] = tie(best, across[3][0])
    jobs = [(0, 4, 0, every), (0, 4, 1, every), (0, 4, 2, every), (0, 4, 3, (0, 2))]
    some = given((0, 2), range(4)) | given((1, 3), range(3))
    (best,) = compare(cap, row, jobs, some, best)
    across[3][-1], best = tie(across[3][-1], best)
    beyond[3] = core(across[3])
    some = given((0,), range(4)) | given((1, 3), (3,))
    best = compare(cap, pieces, [(0, 4, 3, (1, 3))], some, best)
    backs = [exchange(b, low, 1, -1) for b, (low, _) in zip(best, pieces)]
    return unpack(slot, backs).reshape(rows)


def solution(mesh):
    placed = (P(("parts", "blk"), None), P(("parts", "blk")), P(("parts", "blk")))
    return jax.shard_map(
        on_device, mesh=mesh, in_specs=placed, out_specs=P(("parts", "blk")), check_vma=False
    )
```

```python
import jax
import jax.numpy as jnp
from jax import lax
from jax.experimental import pallas as pl
from jax.experimental.pallas import tpu as pltpu
from jax.sharding import PartitionSpec as P

GROUP = 4
BLOCKS = 4
UNITS = (4, 4, 4, 4)
PAD = 16
STEP = 512
GRANT = 16 << 20
NT = (((1,), (1,)), ((), ()))


def iota(shape, axis):
    return lax.broadcasted_iota(jnp.int32, shape, axis)


def spans(widths):
    start, out = 0, []
    for width in widths:
        out.append((start, width))
        start += width
    return out


def pack_kernel(groups, cap, units, emb_hbm, owner_hbm, cluster_hbm, *refs):
    blocks, refs = refs[: len(units)], refs[len(units) :]
    slot_ref, emb_ref, unit_ref, owner_ref, cluster_ref, sems = refs
    rows = emb_ref.shape[0]
    part = rows // 4
    copies = [
        pltpu.make_async_copy(owner_hbm, owner_ref, sems.at[0]),
        pltpu.make_async_copy(cluster_hbm, cluster_ref, sems.at[1]),
    ]
    for i in range(4):
        span = pl.ds(i * part, part)
        copies.append(pltpu.make_async_copy(emb_hbm.at[span], emb_ref.at[span], sems.at[2 + i]))
    for copy in copies:
        copy.start()
    earlier = (iota((rows, rows), 0) < iota((rows, rows), 1)).astype(jnp.bfloat16)
    mine = lax.axis_index("blk") // GROUP
    copies[0].wait()
    rel = ((owner_ref[...] >> 2) - mine + groups) & (groups - 1)
    place = jnp.where(rel > groups // 2, 2 * (groups - rel), jnp.maximum(2 * rel - 1, 0))
    member = iota((max(groups, 16), rows), 0) == place
    count = jnp.dot(member.astype(jnp.bfloat16), earlier, preferred_element_type=jnp.float32)
    rank = jnp.sum(jnp.where(member, count, 0.0), axis=0, keepdims=True)
    slot = place * cap + rank.astype(jnp.int32)
    slot_ref[...] = slot
    copies[1].wait()
    label = ((cluster_ref[...] & 15) + 1).astype(jnp.float32).astype(jnp.bfloat16)
    label = jnp.broadcast_to(label, (PAD, rows))
    for i in range(4):
        copies[2 + i].wait()
        x = emb_ref[i * part : (i + 1) * part, :]
        squares = jnp.sum(x * x, axis=1, keepdims=True)
        unit_ref[i * part : (i + 1) * part, :] = (x * lax.rsqrt(squares + 1e-06)).astype(
            jnp.bfloat16
        )
    unit = unit_ref[...]
    for ref, (start, size) in zip(blocks, units):
        hot = (iota((size, rows), 0) + start == slot).astype(jnp.bfloat16)
        packed = jnp.dot(hot, unit, preferred_element_type=jnp.float32).astype(jnp.bfloat16)
        marks = lax.dot_general(label, hot, NT, preferred_element_type=jnp.float32)
        marks = (marks - 1.0).astype(jnp.bfloat16)
        sub = min(cap, size)
        for i in range(size // sub):
            low = i * (sub + PAD)
            ref[low : low + sub, :] = packed[i * sub : (i + 1) * sub, :]
            ref[low + sub : low + sub + PAD, :] = jnp.zeros((PAD, unit.shape[1]), jnp.bfloat16)
            ref[low + sub : low + sub + PAD, 0:sub] = marks[:, i * sub : (i + 1) * sub]


def pack(groups, cap, units, embedding, owner, cluster):
    rows, width = embedding.shape
    return pl.pallas_call(
        lambda *refs: pack_kernel(groups, cap, units, *refs),
        in_specs=[pl.BlockSpec(memory_space=pltpu.HBM)] * 3,
        out_shape=[
            jax.ShapeDtypeStruct((n + n // min(cap, n) * PAD, width), jnp.bfloat16)
            for _, n in units
        ]
        + [jax.ShapeDtypeStruct((1, rows), jnp.int32)],
        scratch_shapes=[
            pltpu.VMEM((rows, width), jnp.float32),
            pltpu.VMEM((rows, width), jnp.bfloat16),
            pltpu.VMEM((1, rows), jnp.int32),
            pltpu.VMEM((1, rows), jnp.int32),
            pltpu.SemaphoreType.DMA((6,)),
        ],
        name="pack",
    )(embedding, owner.reshape(1, rows), cluster.reshape(1, rows))


def compare_kernel(cap, outs, jobs, names, *refs):
    best_ref, refs = refs[0], refs[1:]
    given = {}
    for name, ref in zip(names, refs):
        given.setdefault(name, []).append(ref)
    refs = refs[len(names) :]
    outputs, scratch = refs[: len(outs)], list(refs[len(outs) :])
    query_ref = scratch.pop()
    size = query_ref.shape[0] // BLOCKS

    def unfold(parts, target, low):
        for ref in parts:
            sub = min(cap, size // len(parts))
            for start in range(0, ref.shape[0], sub + PAD):
                target[low : low + sub, :] = ref[start : start + sub, :]
                low += sub

    keys, marks = {}, {}
    for (peer, k), parts in given.items():
        sub = min(cap, size // len(parts))
        row = [
            ref[start + sub : start + sub + PAD, 0:sub].astype(jnp.float32)
            for ref in parts
            for start in range(0, ref.shape[0], sub + PAD)
        ]
        marks[peer, k] = jnp.concatenate(row, axis=1)[0:1, :]
        if peer == 0:
            unfold(parts, query_ref, k * size)
            keys[peer, k] = query_ref.at[k * size : (k + 1) * size]
        elif size == sub:
            keys[peer, k] = parts[0].at[0:size]
        else:
            keys[peer, k] = scratch.pop()
            unfold(parts, keys[peer, k], 0)
    columns = {}
    for k in range(BLOCKS):
        table = [marks.get((peer, k), marks[0, k]) for peer in range(4)]
        columns[k] = jnp.concatenate(table * 2, axis=0).T
    near = jnp.concatenate([marks[0, k] for k in range(BLOCKS)], axis=1)
    bests = [best_ref[:, k * size : (k + 1) * size] for k in range(BLOCKS)]
    for low, high, k, peers in jobs:
        for left in range(low, high, STEP // size):
            right = min(left + STEP // size, high)
            span = slice(left * size, right * size)
            row = near[0:1, span]
            best = None
            for peer in peers:
                scores = lax.dot_general(
                    keys[peer, k][...],
                    query_ref[span, :],
                    NT,
                    preferred_element_type=jnp.float32,
                )
                allowed = columns[k][:, peer : peer + 1] == row
                if peer == 0 and left <= k < right:
                    shift = (k - left) * size
                    allowed = allowed & (iota(scores.shape, 0) + shift != iota(scores.shape, 1))
                top = jnp.max(jnp.where(allowed, scores, -1.0), axis=0, keepdims=True)
                best = top if best is None else jnp.maximum(best, top)
            for q in range(left, right):
                part = best[:, (q - left) * size : (q - left + 1) * size]
                bests[q] = jnp.maximum(bests[q], part)
    for q in range(BLOCKS):
        spread(outputs, outs, q * size, bests[q])


def spread(refs, outs, start, row):
    for ref, (low, width) in zip(refs, outs):
        a, b = max(low, start), min(low + width, start + row.shape[1])
        if a < b:
            ref[:, a - low : b - low] = row[:, a - start : b - start]


def compare(cap, outs, jobs, blocks, best):
    slots, width = best.shape[1], blocks[0, 0][0].shape[1]
    size = slots // BLOCKS
    tiles = sum((high - low) * len(peers) for low, high, _, peers in jobs)
    folded = [key for key, parts in blocks.items() if key[0] and size > min(cap, size // len(parts))]
    names = tuple(key for key, parts in blocks.items() for _ in parts)
    return pl.pallas_call(
        lambda *refs: compare_kernel(cap, outs, jobs, names, *refs),
        out_shape=[jax.ShapeDtypeStruct((1, n), jnp.float32) for _, n in outs],
        scratch_shapes=[pltpu.VMEM((size, width), jnp.bfloat16)] * len(folded)
        + [pltpu.VMEM((slots, width), jnp.bfloat16)],
        compiler_params=pltpu.CompilerParams(vmem_limit_bytes=GRANT),
        cost_estimate=pl.CostEstimate(
            flops=2 * tiles * size * size * width, bytes_accessed=0, transcendentals=0
        ),
        name=f"compare{len(jobs)}_{tiles}",
    )(best, *[part for parts in blocks.values() for part in parts])


def unpack_kernel(slot_ref, *refs):
    out_ref = refs[-1]
    slot = slot_ref[...]
    rows = slot.shape[1]
    total = jnp.zeros((8, rows), jnp.float32)
    start = 0
    for ref in refs[:-1]:
        size = ref.shape[1]
        column = jnp.broadcast_to(ref[...], (8, size)).T[:, 0:1]
        hit = iota((size, rows), 0) + start == slot
        part = jnp.where(hit, column, 0.0)
        total = total + jnp.sum(part.reshape(size // 8, 8, rows), axis=0)
        start += size
    out_ref[...] = jnp.sum(total, axis=0, keepdims=True)


def unpack(slot, backs):
    return pl.pallas_call(
        unpack_kernel,
        out_shape=jax.ShapeDtypeStruct(slot.shape, jnp.float32),
        compiler_params=pltpu.CompilerParams(vmem_limit_bytes=GRANT),
        name="unpack",
    )(slot, *backs)


def join(parts, axis):
    return parts[0] if len(parts) == 1 else jnp.concatenate(parts, axis=axis)


def on_device(embedding, row_owner, cluster_id):
    rows, _ = embedding.shape
    devices = lax.axis_size("blk")
    groups = devices // GROUP
    cap = GROUP * max(2, 2 * rows // devices)
    slots = groups * cap
    units = spans([slots // 16 * n for n in UNITS])
    pieces = spans([max(cap, 128)] * (slots // max(cap, 128)))
    shifts = [0] + [(k + 1) // 2 if k % 2 else groups - k // 2 for k in range(1, groups)]

    def shift(array, distance):
        step = distance * GROUP
        return lax.ppermute(array, "blk", [(i, (i + step) % devices) for i in range(devices)])

    def swap(array, mask):
        return lax.ppermute(array, "blk", [(i, i ^ mask) for i in range(devices)])

    def exchange(array, start, axis, sign):
        size, out = array.shape[axis], []
        for k in range(start // cap, (start + size - 1) // cap + 1):
            a, b = max(k * cap - start, 0), min((k + 1) * cap - start, size)
            part = lax.slice_in_dim(array, a, b, axis=axis)
            out.append(shift(part, sign * shifts[k]) if shifts[k] else part)
        return join(out, axis)

    *blocks, slot = pack(groups, cap, units, embedding, row_owner, cluster_id)

    def tie(*arrays):
        return lax.optimization_barrier(arrays)

    def send(u):
        (start, size), out = units[u], []
        sub = min(cap, size)
        for i in range(size // sub):
            part = lax.slice_in_dim(blocks[u], i * (sub + PAD), (i + 1) * (sub + PAD))
            distance = shifts[(start + i * sub) // cap]
            out.append(shift(part, distance) if distance else part)
        return join(out, 0)

    def cross(parts):
        return [swap(part, 2) for part in parts]

    def core(parts):
        return [swap(part, 1) for part in parts]

    arrays = [[None] * BLOCKS for _ in range(4)]
    own, across, beside, beyond = arrays
    sent = [blocks[0]] + [send(u) for u in range(1, len(units))]
    own[:] = [sent[0]], [sent[1]], [sent[2]], sent[3:]
    every, row = (0, 1, 2, 3), [(0, slots)]
    floor = jnp.full((1, slots), -1.0, jnp.float32)

    def given(peers, blocks):
        return {(peer, k): arrays[peer][k] for peer in peers for k in blocks}

    if cap == slots // BLOCKS:
        last = [blocks[3]]
        opposite = cross(last)
        diagonal = core(opposite)
        across[0] = cross(own[0])
        own[0], own[1] = tie(own[0], own[1])
        beside[0] = core(own[0])
        for u in (1, 2):
            beside[u], across[u] = core(own[u]), cross(own[u])
        for u in range(3):
            beyond[u] = core(across[u])
        beside[3] = core(own[3])
        some = {(0, k): last for k in range(BLOCKS)} | {(1, 3): opposite, (3, 3): diagonal}
        (source,) = compare(cap, row, [(0, 1, 3, (1, 3))], some, floor)
        some = {(0, k): across[k] for k in range(3)}
        some |= {(0, 3): own[3], (1, 3): own[3], (2, 3): beside[3]}
        (theirs,) = compare(cap, row, [(0, 3, 3, (1, 2))], some, floor)
        mine = swap(theirs, 2)
        some = given(every, range(3)) | {(0, 3): own[0]}
        (best,) = compare(cap, row, [(0, 3, k, every) for k in range(3)], some, floor)
        jobs = [(3, 4, k, every) for k in range(3)] + [(0, 4, 3, (0, 2))]
        some = given(every, range(3)) | given((0, 2), (3,))
        best = list(compare(cap, pieces, jobs, some, best))
        for k in range(3):
            best[k] = jnp.maximum(best[k], mine[:, k * cap : (k + 1) * cap])
        backs = [exchange(b, low, 1, -1) for b, (low, _) in zip(best, pieces)]
        backs[3] = jnp.maximum(backs[3], source[:, :cap])
        return unpack(slot, backs).reshape(rows)

    for u in range(BLOCKS):
        beside[u], across[u] = core(own[u]), cross(own[u])
    for u in range(BLOCKS - 1):
        beyond[u] = core(across[u])

    best = floor
    jobs = [(0, 4, 0, every), (0, 4, 1, every), (0, 4, 2, every), (0, 4, 3, (0, 2))]
    some = given((0, 2), range(4)) | given((1, 3), range(3))
    (best,) = compare(cap, row, jobs, some, best)
    across[3][-1], best = tie(across[3][-1], best)
    beyond[3] = core(across[3])
    some = given((0,), range(4)) | given((1, 3), (3,))
    best = compare(cap, pieces, [(0, 4, 3, (1, 3))], some, best)
    backs = [exchange(b, low, 1, -1) for b, (low, _) in zip(best, pieces)]
    return unpack(slot, backs).reshape(rows)


def solution(mesh):
    placed = (P(("parts", "blk"), None), P(("parts", "blk")), P(("parts", "blk")))
    return jax.shard_map(
        on_device, mesh=mesh, in_specs=placed, out_specs=P(("parts", "blk")), check_vma=False
    )
```

```python
import jax
import jax.numpy as jnp
from jax import lax
from jax.experimental import pallas as pl
from jax.experimental.pallas import tpu as pltpu
from jax.sharding import PartitionSpec as P

GROUP = 4
BLOCKS = 4
UNITS = (4, 4, 4, 4)
PAD = 16
STEP = 512
GRANT = 16 << 20
NT = (((1,), (1,)), ((), ()))


def iota(shape, axis):
    return lax.broadcasted_iota(jnp.int32, shape, axis)


def spans(widths):
    start, out = 0, []
    for width in widths:
        out.append((start, width))
        start += width
    return out


def pack_kernel(groups, cap, units, emb_hbm, owner_hbm, cluster_hbm, *refs):
    blocks, refs = refs[: len(units)], refs[len(units) :]
    slot_ref, emb_ref, unit_ref, owner_ref, cluster_ref, sems = refs
    rows = emb_ref.shape[0]
    part = rows // 4
    copies = [
        pltpu.make_async_copy(owner_hbm, owner_ref, sems.at[0]),
        pltpu.make_async_copy(cluster_hbm, cluster_ref, sems.at[1]),
    ]
    for i in range(4):
        span = pl.ds(i * part, part)
        copies.append(pltpu.make_async_copy(emb_hbm.at[span], emb_ref.at[span], sems.at[2 + i]))
    for copy in copies:
        copy.start()
    earlier = (iota((rows, rows), 0) < iota((rows, rows), 1)).astype(jnp.bfloat16)
    mine = lax.axis_index("blk") // GROUP
    copies[0].wait()
    rel = ((owner_ref[...] >> 2) - mine + groups) & (groups - 1)
    place = jnp.where(rel > groups // 2, 2 * (groups - rel), jnp.maximum(2 * rel - 1, 0))
    member = iota((max(groups, 16), rows), 0) == place
    count = jnp.dot(member.astype(jnp.bfloat16), earlier, preferred_element_type=jnp.float32)
    rank = jnp.sum(jnp.where(member, count, 0.0), axis=0, keepdims=True)
    slot = place * cap + rank.astype(jnp.int32)
    slot_ref[...] = slot
    copies[1].wait()
    label = ((cluster_ref[...] & 15) + 1).astype(jnp.float32).astype(jnp.bfloat16)
    label = jnp.broadcast_to(label, (PAD, rows))
    for i in range(4):
        copies[2 + i].wait()
        x = emb_ref[i * part : (i + 1) * part, :]
        squares = jnp.sum(x * x, axis=1, keepdims=True)
        unit_ref[i * part : (i + 1) * part, :] = (x * lax.rsqrt(squares + 1e-06)).astype(
            jnp.bfloat16
        )
    unit = unit_ref[...]
    for ref, (start, size) in zip(blocks, units):
        hot = (iota((size, rows), 0) + start == slot).astype(jnp.bfloat16)
        packed = jnp.dot(hot, unit, preferred_element_type=jnp.float32).astype(jnp.bfloat16)
        marks = lax.dot_general(label, hot, NT, preferred_element_type=jnp.float32)
        marks = (marks - 1.0).astype(jnp.bfloat16)
        sub = min(cap, size)
        for i in range(size // sub):
            low = i * (sub + PAD)
            ref[low : low + sub, :] = packed[i * sub : (i + 1) * sub, :]
            ref[low + sub : low + sub + PAD, :] = jnp.zeros((PAD, unit.shape[1]), jnp.bfloat16)
            ref[low + sub : low + sub + PAD, 0:sub] = marks[:, i * sub : (i + 1) * sub]


def pack(groups, cap, units, embedding, owner, cluster):
    rows, width = embedding.shape
    return pl.pallas_call(
        lambda *refs: pack_kernel(groups, cap, units, *refs),
        in_specs=[pl.BlockSpec(memory_space=pltpu.HBM)] * 3,
        out_shape=[
            jax.ShapeDtypeStruct((n + n // min(cap, n) * PAD, width), jnp.bfloat16)
            for _, n in units
        ]
        + [jax.ShapeDtypeStruct((1, rows), jnp.int32)],
        scratch_shapes=[
            pltpu.VMEM((rows, width), jnp.float32),
            pltpu.VMEM((rows, width), jnp.bfloat16),
            pltpu.VMEM((1, rows), jnp.int32),
            pltpu.VMEM((1, rows), jnp.int32),
            pltpu.SemaphoreType.DMA((6,)),
        ],
        name="pack",
    )(embedding, owner.reshape(1, rows), cluster.reshape(1, rows))


def compare_kernel(cap, outs, jobs, names, *refs):
    best_ref, refs = refs[0], refs[1:]
    given = {}
    for name, ref in zip(names, refs):
        given.setdefault(name, []).append(ref)
    refs = refs[len(names) :]
    outputs, scratch = refs[: len(outs)], list(refs[len(outs) :])
    query_ref = scratch.pop()
    size = query_ref.shape[0] // BLOCKS

    def unfold(parts, target, low):
        for ref in parts:
            sub = min(cap, size // len(parts))
            for start in range(0, ref.shape[0], sub + PAD):
                target[low : low + sub, :] = ref[start : start + sub, :]
                low += sub

    keys, marks = {}, {}
    for (peer, k), parts in given.items():
        sub = min(cap, size // len(parts))
        row = [
            ref[start + sub : start + sub + PAD, 0:sub].astype(jnp.float32)
            for ref in parts
            for start in range(0, ref.shape[0], sub + PAD)
        ]
        marks[peer, k] = jnp.concatenate(row, axis=1)[0:1, :]
        if peer == 0:
            unfold(parts, query_ref, k * size)
            keys[peer, k] = query_ref.at[k * size : (k + 1) * size]
        elif size == sub:
            keys[peer, k] = parts[0].at[0:size]
        else:
            keys[peer, k] = scratch.pop()
            unfold(parts, keys[peer, k], 0)
    columns = {}
    for k in range(BLOCKS):
        table = [marks.get((peer, k), marks[0, k]) for peer in range(4)]
        columns[k] = jnp.concatenate(table * 2, axis=0).T
    near = jnp.concatenate([marks[0, k] for k in range(BLOCKS)], axis=1)
    bests = [best_ref[:, k * size : (k + 1) * size] for k in range(BLOCKS)]
    for low, high, k, peers in jobs:
        for left in range(low, high, STEP // size):
            right = min(left + STEP // size, high)
            span = slice(left * size, right * size)
            row = near[0:1, span]
            best = None
            for peer in peers:
                scores = lax.dot_general(
                    keys[peer, k][...],
                    query_ref[span, :],
                    NT,
                    preferred_element_type=jnp.float32,
                )
                allowed = columns[k][:, peer : peer + 1] == row
                if peer == 0 and left <= k < right:
                    shift = (k - left) * size
                    allowed = allowed & (iota(scores.shape, 0) + shift != iota(scores.shape, 1))
                top = jnp.max(jnp.where(allowed, scores, -1.0), axis=0, keepdims=True)
                best = top if best is None else jnp.maximum(best, top)
            for q in range(left, right):
                part = best[:, (q - left) * size : (q - left + 1) * size]
                bests[q] = jnp.maximum(bests[q], part)
    for q in range(BLOCKS):
        spread(outputs, outs, q * size, bests[q])


def spread(refs, outs, start, row):
    for ref, (low, width) in zip(refs, outs):
        a, b = max(low, start), min(low + width, start + row.shape[1])
        if a < b:
            ref[:, a - low : b - low] = row[:, a - start : b - start]


def compare(cap, outs, jobs, blocks, best):
    slots, width = best.shape[1], blocks[0, 0][0].shape[1]
    size = slots // BLOCKS
    tiles = sum((high - low) * len(peers) for low, high, _, peers in jobs)
    folded = [key for key, parts in blocks.items() if key[0] and size > min(cap, size // len(parts))]
    names = tuple(key for key, parts in blocks.items() for _ in parts)
    return pl.pallas_call(
        lambda *refs: compare_kernel(cap, outs, jobs, names, *refs),
        out_shape=[jax.ShapeDtypeStruct((1, n), jnp.float32) for _, n in outs],
        scratch_shapes=[pltpu.VMEM((size, width), jnp.bfloat16)] * len(folded)
        + [pltpu.VMEM((slots, width), jnp.bfloat16)],
        compiler_params=pltpu.CompilerParams(vmem_limit_bytes=GRANT),
        cost_estimate=pl.CostEstimate(
            flops=2 * tiles * size * size * width, bytes_accessed=0, transcendentals=0
        ),
        name=f"compare{len(jobs)}_{tiles}",
    )(best, *[part for parts in blocks.values() for part in parts])


def unpack_kernel(slot_ref, *refs):
    out_ref = refs[-1]
    slot = slot_ref[...]
    rows = slot.shape[1]
    total = jnp.zeros((8, rows), jnp.float32)
    start = 0
    for ref in refs[:-1]:
        size = ref.shape[1]
        column = jnp.broadcast_to(ref[...], (8, size)).T[:, 0:1]
        hit = iota((size, rows), 0) + start == slot
        part = jnp.where(hit, column, 0.0)
        total = total + jnp.sum(part.reshape(size // 8, 8, rows), axis=0)
        start += size
    out_ref[...] = jnp.sum(total, axis=0, keepdims=True)


def unpack(slot, backs):
    return pl.pallas_call(
        unpack_kernel,
        out_shape=jax.ShapeDtypeStruct(slot.shape, jnp.float32),
        compiler_params=pltpu.CompilerParams(vmem_limit_bytes=GRANT),
        name="unpack",
    )(slot, *backs)


def join(parts, axis):
    return parts[0] if len(parts) == 1 else jnp.concatenate(parts, axis=axis)


def on_device(embedding, row_owner, cluster_id):
    rows, _ = embedding.shape
    devices = lax.axis_size("blk")
    groups = devices // GROUP
    cap = GROUP * max(2, 2 * rows // devices)
    slots = groups * cap
    units = spans([slots // 16 * n for n in UNITS])
    pieces = spans([max(cap, 128)] * (slots // max(cap, 128)))
    shifts = [0] + [(k + 1) // 2 if k % 2 else groups - k // 2 for k in range(1, groups)]

    def shift(array, distance):
        step = distance * GROUP
        return lax.ppermute(array, "blk", [(i, (i + step) % devices) for i in range(devices)])

    def swap(array, mask):
        return lax.ppermute(array, "blk", [(i, i ^ mask) for i in range(devices)])

    def exchange(array, start, axis, sign):
        size, out = array.shape[axis], []
        for k in range(start // cap, (start + size - 1) // cap + 1):
            a, b = max(k * cap - start, 0), min((k + 1) * cap - start, size)
            part = lax.slice_in_dim(array, a, b, axis=axis)
            out.append(shift(part, sign * shifts[k]) if shifts[k] else part)
        return join(out, axis)

    *blocks, slot = pack(groups, cap, units, embedding, row_owner, cluster_id)

    def tie(*arrays):
        return lax.optimization_barrier(arrays)

    def send(u):
        (start, size), out = units[u], []
        sub = min(cap, size)
        for i in range(size // sub):
            part = lax.slice_in_dim(blocks[u], i * (sub + PAD), (i + 1) * (sub + PAD))
            distance = shifts[(start + i * sub) // cap]
            out.append(shift(part, distance) if distance else part)
        return join(out, 0)

    def cross(parts):
        return [swap(part, 2) for part in parts]

    def core(parts):
        return [swap(part, 1) for part in parts]

    arrays = [[None] * BLOCKS for _ in range(4)]
    own, across, beside, beyond = arrays
    sent = [blocks[0], send(1)]
    heads = blocks[2], blocks[3]
    *heads, sent[1] = tie(*heads, sent[1])
    last = [blocks[3]]
    blocks[2:] = heads
    sent += [send(2), send(3)]
    own[:] = [sent[0]], [sent[1]], [sent[2]], sent[3:]
    every, row = (0, 1, 2, 3), [(0, slots)]
    floor = jnp.full((1, slots), -1.0, jnp.float32)

    def given(peers, blocks):
        return {(peer, k): arrays[peer][k] for peer in peers for k in blocks}

    if cap == slots // BLOCKS:
        opposite = cross(last)
        diagonal = core(opposite)
        across[0] = cross(own[0])
        own[0], own[1] = tie(own[0], own[1])
        beside[0] = core(own[0])
        for u in (1, 2):
            beside[u], across[u] = core(own[u]), cross(own[u])
        for u in range(3):
            beyond[u] = core(across[u])
        beside[3] = core(own[3])
        some = {(0, k): last for k in range(BLOCKS)} | {(1, 3): opposite, (3, 3): diagonal}
        (source,) = compare(cap, row, [(0, 1, 3, (1, 3))], some, floor)
        some = {(0, k): across[k] for k in range(3)}
        some |= {(0, 3): own[3], (1, 3): own[3], (2, 3): beside[3]}
        (theirs,) = compare(cap, row, [(0, 3, 3, (1, 2))], some, floor)
        mine = swap(theirs, 2)
        some = given(every, range(3)) | {(0, 3): own[0]}
        (best,) = compare(cap, row, [(0, 3, k, every) for k in range(3)], some, floor)
        jobs = [(3, 4, k, every) for k in range(3)] + [(0, 4, 3, (0, 2))]
        some = given(every, range(3)) | given((0, 2), (3,))
        best = list(compare(cap, pieces, jobs, some, best))
        for k in range(3):
            best[k] = jnp.maximum(best[k], mine[:, k * cap : (k + 1) * cap])
        backs = [exchange(b, low, 1, -1) for b, (low, _) in zip(best, pieces)]
        backs[3] = jnp.maximum(backs[3], source[:, :cap])
        return unpack(slot, backs).reshape(rows)

    for u in range(BLOCKS):
        beside[u], across[u] = core(own[u]), cross(own[u])
    for u in range(BLOCKS - 1):
        beyond[u] = core(across[u])

    best = floor
    jobs = [(0, 4, 0, every), (0, 4, 1, every), (0, 4, 2, every), (0, 4, 3, (0, 2))]
    some = given((0, 2), range(4)) | given((1, 3), range(3))
    (best,) = compare(cap, row, jobs, some, best)
    across[3][-1], best = tie(across[3][-1], best)
    beyond[3] = core(across[3])
    some = given((0,), range(4)) | given((1, 3), (3,))
    best = compare(cap, pieces, [(0, 4, 3, (1, 3))], some, best)
    backs = [exchange(b, low, 1, -1) for b, (low, _) in zip(best, pieces)]
    return unpack(slot, backs).reshape(rows)


def solution(mesh):
    placed = (P(("parts", "blk"), None), P(("parts", "blk")), P(("parts", "blk")))
    return jax.shard_map(
        on_device, mesh=mesh, in_specs=placed, out_specs=P(("parts", "blk")), check_vma=False
    )
```

```python
import jax
import jax.numpy as jnp
from jax import lax
from jax.experimental import pallas as pl
from jax.experimental.pallas import tpu as pltpu
from jax.sharding import PartitionSpec as P

GROUP = 4
BLOCKS = 4
UNITS = (4, 4, 4, 4)
PAD = 16
STEP = 512
GRANT = 16 << 20
NT = (((1,), (1,)), ((), ()))


def iota(shape, axis):
    return lax.broadcasted_iota(jnp.int32, shape, axis)


def spans(widths):
    start, out = 0, []
    for width in widths:
        out.append((start, width))
        start += width
    return out


def pack_kernel(groups, cap, units, emb_hbm, owner_hbm, cluster_hbm, *refs):
    blocks, refs = refs[: len(units)], refs[len(units) :]
    slot_ref, emb_ref, unit_ref, owner_ref, cluster_ref, sems = refs
    rows = emb_ref.shape[0]
    part = rows // 4
    copies = [
        pltpu.make_async_copy(owner_hbm, owner_ref, sems.at[0]),
        pltpu.make_async_copy(cluster_hbm, cluster_ref, sems.at[1]),
    ]
    for i in range(4):
        span = pl.ds(i * part, part)
        copies.append(pltpu.make_async_copy(emb_hbm.at[span], emb_ref.at[span], sems.at[2 + i]))
    for copy in copies:
        copy.start()
    earlier = (iota((rows, rows), 0) < iota((rows, rows), 1)).astype(jnp.bfloat16)
    mine = lax.axis_index("blk") // GROUP
    copies[0].wait()
    rel = ((owner_ref[...] >> 2) - mine + groups) & (groups - 1)
    place = jnp.where(rel > groups // 2, 2 * (groups - rel), jnp.maximum(2 * rel - 1, 0))
    member = iota((max(groups, 16), rows), 0) == place
    count = jnp.dot(member.astype(jnp.bfloat16), earlier, preferred_element_type=jnp.float32)
    rank = jnp.sum(jnp.where(member, count, 0.0), axis=0, keepdims=True)
    slot = place * cap + rank.astype(jnp.int32)
    slot_ref[...] = slot
    copies[1].wait()
    label = ((cluster_ref[...] & 15) + 1).astype(jnp.float32).astype(jnp.bfloat16)
    label = jnp.broadcast_to(label, (PAD, rows))
    for i in range(4):
        copies[2 + i].wait()
        x = emb_ref[i * part : (i + 1) * part, :]
        squares = jnp.sum(x * x, axis=1, keepdims=True)
        unit_ref[i * part : (i + 1) * part, :] = (x * lax.rsqrt(squares + 1e-06)).astype(
            jnp.bfloat16
        )
    unit = unit_ref[...]
    for ref, (start, size) in zip(blocks, units):
        hot = (iota((size, rows), 0) + start == slot).astype(jnp.bfloat16)
        packed = jnp.dot(hot, unit, preferred_element_type=jnp.float32).astype(jnp.bfloat16)
        marks = lax.dot_general(label, hot, NT, preferred_element_type=jnp.float32)
        marks = (marks - 1.0).astype(jnp.bfloat16)
        sub = min(cap, size)
        for i in range(size // sub):
            low = i * (sub + PAD)
            ref[low : low + sub, :] = packed[i * sub : (i + 1) * sub, :]
            ref[low + sub : low + sub + PAD, :] = jnp.zeros((PAD, unit.shape[1]), jnp.bfloat16)
            ref[low + sub : low + sub + PAD, 0:sub] = marks[:, i * sub : (i + 1) * sub]


def pack(groups, cap, units, embedding, owner, cluster):
    rows, width = embedding.shape
    return pl.pallas_call(
        lambda *refs: pack_kernel(groups, cap, units, *refs),
        in_specs=[pl.BlockSpec(memory_space=pltpu.HBM)] * 3,
        out_shape=[
            jax.ShapeDtypeStruct((n + n // min(cap, n) * PAD, width), jnp.bfloat16)
            for _, n in units
        ]
        + [jax.ShapeDtypeStruct((1, rows), jnp.int32)],
        scratch_shapes=[
            pltpu.VMEM((rows, width), jnp.float32),
            pltpu.VMEM((rows, width), jnp.bfloat16),
            pltpu.VMEM((1, rows), jnp.int32),
            pltpu.VMEM((1, rows), jnp.int32),
            pltpu.SemaphoreType.DMA((6,)),
        ],
        name="pack",
    )(embedding, owner.reshape(1, rows), cluster.reshape(1, rows))


def compare_kernel(cap, outs, jobs, names, *refs):
    best_ref, refs = refs[0], refs[1:]
    given = {}
    for name, ref in zip(names, refs):
        given.setdefault(name, []).append(ref)
    refs = refs[len(names) :]
    outputs, scratch = refs[: len(outs)], list(refs[len(outs) :])
    query_ref = scratch.pop()
    size = query_ref.shape[0] // BLOCKS

    def unfold(parts, target, low):
        for ref in parts:
            sub = min(cap, size // len(parts))
            for start in range(0, ref.shape[0], sub + PAD):
                target[low : low + sub, :] = ref[start : start + sub, :]
                low += sub

    keys, marks = {}, {}
    for (peer, k), parts in given.items():
        sub = min(cap, size // len(parts))
        row = [
            ref[start + sub : start + sub + PAD, 0:sub].astype(jnp.float32)
            for ref in parts
            for start in range(0, ref.shape[0], sub + PAD)
        ]
        marks[peer, k] = jnp.concatenate(row, axis=1)[0:1, :]
        if peer == 0:
            unfold(parts, query_ref, k * size)
            keys[peer, k] = query_ref.at[k * size : (k + 1) * size]
        elif size == sub:
            keys[peer, k] = parts[0].at[0:size]
        else:
            keys[peer, k] = scratch.pop()
            unfold(parts, keys[peer, k], 0)
    columns = {}
    for k in range(BLOCKS):
        table = [marks.get((peer, k), marks[0, k]) for peer in range(4)]
        columns[k] = jnp.concatenate(table * 2, axis=0).T
    near = jnp.concatenate([marks[0, k] for k in range(BLOCKS)], axis=1)
    bests = [best_ref[:, k * size : (k + 1) * size] for k in range(BLOCKS)]
    for low, high, k, peers in jobs:
        for left in range(low, high, STEP // size):
            right = min(left + STEP // size, high)
            span = slice(left * size, right * size)
            row = near[0:1, span]
            best = None
            for peer in peers:
                scores = lax.dot_general(
                    keys[peer, k][...],
                    query_ref[span, :],
                    NT,
                    preferred_element_type=jnp.float32,
                )
                allowed = columns[k][:, peer : peer + 1] == row
                if peer == 0 and left <= k < right:
                    shift = (k - left) * size
                    allowed = allowed & (iota(scores.shape, 0) + shift != iota(scores.shape, 1))
                top = jnp.max(jnp.where(allowed, scores, -1.0), axis=0, keepdims=True)
                best = top if best is None else jnp.maximum(best, top)
            for q in range(left, right):
                part = best[:, (q - left) * size : (q - left + 1) * size]
                bests[q] = jnp.maximum(bests[q], part)
    for q in range(BLOCKS):
        spread(outputs, outs, q * size, bests[q])


def spread(refs, outs, start, row):
    for ref, (low, width) in zip(refs, outs):
        a, b = max(low, start), min(low + width, start + row.shape[1])
        if a < b:
            ref[:, a - low : b - low] = row[:, a - start : b - start]


def compare(cap, outs, jobs, blocks, best):
    slots, width = best.shape[1], blocks[0, 0][0].shape[1]
    size = slots // BLOCKS
    tiles = sum((high - low) * len(peers) for low, high, _, peers in jobs)
    folded = [key for key, parts in blocks.items() if key[0] and size > min(cap, size // len(parts))]
    names = tuple(key for key, parts in blocks.items() for _ in parts)
    return pl.pallas_call(
        lambda *refs: compare_kernel(cap, outs, jobs, names, *refs),
        out_shape=[jax.ShapeDtypeStruct((1, n), jnp.float32) for _, n in outs],
        scratch_shapes=[pltpu.VMEM((size, width), jnp.bfloat16)] * len(folded)
        + [pltpu.VMEM((slots, width), jnp.bfloat16)],
        compiler_params=pltpu.CompilerParams(vmem_limit_bytes=GRANT),
        cost_estimate=pl.CostEstimate(
            flops=2 * tiles * size * size * width, bytes_accessed=0, transcendentals=0
        ),
        name=f"compare{len(jobs)}_{tiles}",
    )(best, *[part for parts in blocks.values() for part in parts])


def unpack_kernel(slot_ref, *refs):
    out_ref = refs[-1]
    slot = slot_ref[...]
    rows = slot.shape[1]
    total = jnp.zeros((8, rows), jnp.float32)
    start = 0
    for ref in refs[:-1]:
        size = ref.shape[1]
        column = jnp.broadcast_to(ref[...], (8, size)).T[:, 0:1]
        hit = iota((size, rows), 0) + start == slot
        part = jnp.where(hit, column, 0.0)
        total = total + jnp.sum(part.reshape(size // 8, 8, rows), axis=0)
        start += size
    out_ref[...] = jnp.sum(total, axis=0, keepdims=True)


def unpack(slot, backs):
    return pl.pallas_call(
        unpack_kernel,
        out_shape=jax.ShapeDtypeStruct(slot.shape, jnp.float32),
        compiler_params=pltpu.CompilerParams(vmem_limit_bytes=GRANT),
        name="unpack",
    )(slot, *backs)


def join(parts, axis):
    return parts[0] if len(parts) == 1 else jnp.concatenate(parts, axis=axis)


def on_device(embedding, row_owner, cluster_id):
    rows, _ = embedding.shape
    devices = lax.axis_size("blk")
    groups = devices // GROUP
    cap = GROUP * max(2, 2 * rows // devices)
    slots = groups * cap
    units = spans([slots // 16 * n for n in UNITS])
    pieces = spans([max(cap, 128)] * (slots // max(cap, 128)))
    shifts = [0] + [(k + 1) // 2 if k % 2 else groups - k // 2 for k in range(1, groups)]

    def shift(array, distance):
        step = distance * GROUP
        return lax.ppermute(array, "blk", [(i, (i + step) % devices) for i in range(devices)])

    def swap(array, mask):
        return lax.ppermute(array, "blk", [(i, i ^ mask) for i in range(devices)])

    def exchange(array, start, axis, sign):
        size, out = array.shape[axis], []
        for k in range(start // cap, (start + size - 1) // cap + 1):
            a, b = max(k * cap - start, 0), min((k + 1) * cap - start, size)
            part = lax.slice_in_dim(array, a, b, axis=axis)
            out.append(shift(part, sign * shifts[k]) if shifts[k] else part)
        return join(out, axis)

    *blocks, slot = pack(groups, cap, units, embedding, row_owner, cluster_id)

    def tie(*arrays):
        return lax.optimization_barrier(arrays)

    def send(u):
        (start, size), out = units[u], []
        sub = min(cap, size)
        for i in range(size // sub):
            part = lax.slice_in_dim(blocks[u], i * (sub + PAD), (i + 1) * (sub + PAD))
            distance = shifts[(start + i * sub) // cap]
            out.append(shift(part, distance) if distance else part)
        return join(out, 0)

    def cross(parts):
        return [swap(part, 2) for part in parts]

    def core(parts):
        return [swap(part, 1) for part in parts]

    arrays = [[None] * BLOCKS for _ in range(4)]
    own, across, beside, beyond = arrays
    sent = [blocks[0], send(1)]
    heads = blocks[2], blocks[3]
    *heads, sent[1] = tie(*heads, sent[1])
    last = [blocks[3]]
    blocks[2:] = heads
    sent += [send(2), send(3)]
    own[:] = [sent[0]], [sent[1]], [sent[2]], sent[3:]
    every, row = (0, 1, 2, 3), [(0, slots)]
    floor = jnp.full((1, slots), -1.0, jnp.float32)

    def given(peers, blocks):
        return {(peer, k): arrays[peer][k] for peer in peers for k in blocks}

    if cap == slots // BLOCKS:
        opposite = cross(last)
        diagonal = core(opposite)
        across[0] = cross(own[0])
        own[0], own[1] = tie(own[0], own[1])
        beside[0] = core(own[0])
        some = {(0, k): last for k in range(BLOCKS)} | {(1, 3): opposite, (3, 3): diagonal}
        (source,) = compare(cap, row, [(0, 1, 3, (1, 3))], some, floor)
        for u in (1, 2):
            beside[u] = core(own[u])
            if u == 2:
                own[2][0], source = tie(own[2][0], source)
            across[u] = cross(own[u])
        for u in range(3):
            beyond[u] = core(across[u])
        beside[3] = core(own[3])
        some = {(0, k): across[k] for k in range(3)}
        some |= {(0, 3): own[3], (1, 3): own[3], (2, 3): beside[3]}
        (theirs,) = compare(cap, row, [(0, 3, 3, (1, 2))], some, floor)
        mine = swap(theirs, 2)
        some = given(every, range(3)) | {(0, 3): own[0]}
        (best,) = compare(cap, row, [(0, 3, k, every) for k in range(3)], some, floor)
        jobs = [(3, 4, k, every) for k in range(3)] + [(0, 4, 3, (0, 2))]
        some = given(every, range(3)) | given((0, 2), (3,))
        best = list(compare(cap, pieces, jobs, some, best))
        for k in range(3):
            best[k] = jnp.maximum(best[k], mine[:, k * cap : (k + 1) * cap])
        backs = [exchange(b, low, 1, -1) for b, (low, _) in zip(best, pieces)]
        backs[3] = jnp.maximum(backs[3], source[:, :cap])
        return unpack(slot, backs).reshape(rows)

    for u in range(BLOCKS):
        beside[u], across[u] = core(own[u]), cross(own[u])
    for u in range(BLOCKS - 1):
        beyond[u] = core(across[u])

    best = floor
    jobs = [(0, 4, 0, every), (0, 4, 1, every), (0, 4, 2, every), (0, 4, 3, (0, 2))]
    some = given((0, 2), range(4)) | given((1, 3), range(3))
    (best,) = compare(cap, row, jobs, some, best)
    across[3][-1], best = tie(across[3][-1], best)
    beyond[3] = core(across[3])
    some = given((0,), range(4)) | given((1, 3), (3,))
    best = compare(cap, pieces, [(0, 4, 3, (1, 3))], some, best)
    backs = [exchange(b, low, 1, -1) for b, (low, _) in zip(best, pieces)]
    return unpack(slot, backs).reshape(rows)


def solution(mesh):
    placed = (P(("parts", "blk"), None), P(("parts", "blk")), P(("parts", "blk")))
    return jax.shard_map(
        on_device, mesh=mesh, in_specs=placed, out_specs=P(("parts", "blk")), check_vma=False
    )
```

```python
import jax
import jax.numpy as jnp
from jax import lax
from jax.experimental import pallas as pl
from jax.experimental.pallas import tpu as pltpu
from jax.sharding import PartitionSpec as P

GROUP = 4
BLOCKS = 4
UNITS = (4, 4, 4, 4)
PAD = 16
STEP = 512
GRANT = 16 << 20
NT = (((1,), (1,)), ((), ()))


def iota(shape, axis):
    return lax.broadcasted_iota(jnp.int32, shape, axis)


def spans(widths):
    start, out = 0, []
    for width in widths:
        out.append((start, width))
        start += width
    return out


def pack_kernel(groups, cap, units, emb_hbm, owner_hbm, cluster_hbm, *refs):
    blocks, refs = refs[: len(units)], refs[len(units) :]
    slot_ref, emb_ref, unit_ref, owner_ref, cluster_ref, sems = refs
    rows = emb_ref.shape[0]
    part = rows // 4
    copies = [
        pltpu.make_async_copy(owner_hbm, owner_ref, sems.at[0]),
        pltpu.make_async_copy(cluster_hbm, cluster_ref, sems.at[1]),
    ]
    for i in range(4):
        span = pl.ds(i * part, part)
        copies.append(pltpu.make_async_copy(emb_hbm.at[span], emb_ref.at[span], sems.at[2 + i]))
    for copy in copies:
        copy.start()
    earlier = (iota((rows, rows), 0) < iota((rows, rows), 1)).astype(jnp.bfloat16)
    mine = lax.axis_index("blk") // GROUP
    copies[0].wait()
    rel = ((owner_ref[...] >> 2) - mine + groups) & (groups - 1)
    place = jnp.where(rel > groups // 2, 2 * (groups - rel), jnp.maximum(2 * rel - 1, 0))
    member = iota((max(groups, 16), rows), 0) == place
    count = jnp.dot(member.astype(jnp.bfloat16), earlier, preferred_element_type=jnp.float32)
    rank = jnp.sum(jnp.where(member, count, 0.0), axis=0, keepdims=True)
    slot = place * cap + rank.astype(jnp.int32)
    slot_ref[...] = slot
    copies[1].wait()
    label = ((cluster_ref[...] & 15) + 1).astype(jnp.float32).astype(jnp.bfloat16)
    label = jnp.broadcast_to(label, (PAD, rows))
    for i in range(4):
        copies[2 + i].wait()
        x = emb_ref[i * part : (i + 1) * part, :]
        squares = jnp.sum(x * x, axis=1, keepdims=True)
        unit_ref[i * part : (i + 1) * part, :] = (x * lax.rsqrt(squares + 1e-06)).astype(
            jnp.bfloat16
        )
    unit = unit_ref[...]
    for ref, (start, size) in zip(blocks, units):
        hot = (iota((size, rows), 0) + start == slot).astype(jnp.bfloat16)
        packed = jnp.dot(hot, unit, preferred_element_type=jnp.float32).astype(jnp.bfloat16)
        marks = lax.dot_general(label, hot, NT, preferred_element_type=jnp.float32)
        marks = (marks - 1.0).astype(jnp.bfloat16)
        sub = min(cap, size)
        for i in range(size // sub):
            low = i * (sub + PAD)
            ref[low : low + sub, :] = packed[i * sub : (i + 1) * sub, :]
            ref[low + sub : low + sub + PAD, :] = jnp.zeros((PAD, unit.shape[1]), jnp.bfloat16)
            ref[low + sub : low + sub + PAD, 0:sub] = marks[:, i * sub : (i + 1) * sub]


def pack(groups, cap, units, embedding, owner, cluster):
    rows, width = embedding.shape
    return pl.pallas_call(
        lambda *refs: pack_kernel(groups, cap, units, *refs),
        in_specs=[pl.BlockSpec(memory_space=pltpu.HBM)] * 3,
        out_shape=[
            jax.ShapeDtypeStruct((n + n // min(cap, n) * PAD, width), jnp.bfloat16)
            for _, n in units
        ]
        + [jax.ShapeDtypeStruct((1, rows), jnp.int32)],
        scratch_shapes=[
            pltpu.VMEM((rows, width), jnp.float32),
            pltpu.VMEM((rows, width), jnp.bfloat16),
            pltpu.VMEM((1, rows), jnp.int32),
            pltpu.VMEM((1, rows), jnp.int32),
            pltpu.SemaphoreType.DMA((6,)),
        ],
        name="pack",
    )(embedding, owner.reshape(1, rows), cluster.reshape(1, rows))


def compare_kernel(cap, outs, jobs, names, *refs):
    best_ref, refs = refs[0], refs[1:]
    given = {}
    for name, ref in zip(names, refs):
        given.setdefault(name, []).append(ref)
    refs = refs[len(names) :]
    outputs, scratch = refs[: len(outs)], list(refs[len(outs) :])
    query_ref = scratch.pop()
    size = query_ref.shape[0] // BLOCKS

    def unfold(parts, target, low):
        for ref in parts:
            sub = min(cap, size // len(parts))
            for start in range(0, ref.shape[0], sub + PAD):
                target[low : low + sub, :] = ref[start : start + sub, :]
                low += sub

    keys, marks = {}, {}
    for (peer, k), parts in given.items():
        sub = min(cap, size // len(parts))
        row = [
            ref[start + sub : start + sub + PAD, 0:sub].astype(jnp.float32)
            for ref in parts
            for start in range(0, ref.shape[0], sub + PAD)
        ]
        marks[peer, k] = jnp.concatenate(row, axis=1)[0:1, :]
        if peer == 0:
            unfold(parts, query_ref, k * size)
            keys[peer, k] = query_ref.at[k * size : (k + 1) * size]
        elif size == sub:
            keys[peer, k] = parts[0].at[0:size]
        else:
            keys[peer, k] = scratch.pop()
            unfold(parts, keys[peer, k], 0)
    columns = {}
    for k in range(BLOCKS):
        table = [marks.get((peer, k), marks[0, k]) for peer in range(4)]
        columns[k] = jnp.concatenate(table * 2, axis=0).T
    near = jnp.concatenate([marks[0, k] for k in range(BLOCKS)], axis=1)
    bests = [best_ref[:, k * size : (k + 1) * size] for k in range(BLOCKS)]
    for low, high, k, peers in jobs:
        for left in range(low, high, STEP // size):
            right = min(left + STEP // size, high)
            span = slice(left * size, right * size)
            row = near[0:1, span]
            best = None
            for peer in peers:
                scores = lax.dot_general(
                    keys[peer, k][...],
                    query_ref[span, :],
                    NT,
                    preferred_element_type=jnp.float32,
                )
                allowed = columns[k][:, peer : peer + 1] == row
                if peer == 0 and left <= k < right:
                    shift = (k - left) * size
                    allowed = allowed & (iota(scores.shape, 0) + shift != iota(scores.shape, 1))
                top = jnp.max(jnp.where(allowed, scores, -1.0), axis=0, keepdims=True)
                best = top if best is None else jnp.maximum(best, top)
            for q in range(left, right):
                part = best[:, (q - left) * size : (q - left + 1) * size]
                bests[q] = jnp.maximum(bests[q], part)
    for q in range(BLOCKS):
        spread(outputs, outs, q * size, bests[q])


def spread(refs, outs, start, row):
    for ref, (low, width) in zip(refs, outs):
        a, b = max(low, start), min(low + width, start + row.shape[1])
        if a < b:
            ref[:, a - low : b - low] = row[:, a - start : b - start]


def compare(cap, outs, jobs, blocks, best):
    slots, width = best.shape[1], blocks[0, 0][0].shape[1]
    size = slots // BLOCKS
    tiles = sum((high - low) * len(peers) for low, high, _, peers in jobs)
    folded = [key for key, parts in blocks.items() if key[0] and size > min(cap, size // len(parts))]
    names = tuple(key for key, parts in blocks.items() for _ in parts)
    return pl.pallas_call(
        lambda *refs: compare_kernel(cap, outs, jobs, names, *refs),
        out_shape=[jax.ShapeDtypeStruct((1, n), jnp.float32) for _, n in outs],
        scratch_shapes=[pltpu.VMEM((size, width), jnp.bfloat16)] * len(folded)
        + [pltpu.VMEM((slots, width), jnp.bfloat16)],
        compiler_params=pltpu.CompilerParams(vmem_limit_bytes=GRANT),
        cost_estimate=pl.CostEstimate(
            flops=2 * tiles * size * size * width, bytes_accessed=0, transcendentals=0
        ),
        name=f"compare{len(jobs)}_{tiles}",
    )(best, *[part for parts in blocks.values() for part in parts])


def unpack_kernel(slot_ref, *refs):
    out_ref = refs[-1]
    slot = slot_ref[...]
    rows = slot.shape[1]
    total = jnp.zeros((8, rows), jnp.float32)
    start = 0
    for ref in refs[:-1]:
        size = ref.shape[1]
        column = jnp.broadcast_to(ref[...], (8, size)).T[:, 0:1]
        hit = iota((size, rows), 0) + start == slot
        part = jnp.where(hit, column, 0.0)
        total = total + jnp.sum(part.reshape(size // 8, 8, rows), axis=0)
        start += size
    out_ref[...] = jnp.sum(total, axis=0, keepdims=True)


def unpack(slot, backs):
    return pl.pallas_call(
        unpack_kernel,
        out_shape=jax.ShapeDtypeStruct(slot.shape, jnp.float32),
        compiler_params=pltpu.CompilerParams(vmem_limit_bytes=GRANT),
        name="unpack",
    )(slot, *backs)


def join(parts, axis):
    return parts[0] if len(parts) == 1 else jnp.concatenate(parts, axis=axis)


def on_device(embedding, row_owner, cluster_id):
    rows, _ = embedding.shape
    devices = lax.axis_size("blk")
    groups = devices // GROUP
    cap = GROUP * max(2, 2 * rows // devices)
    slots = groups * cap
    units = spans([slots // 16 * n for n in UNITS])
    pieces = spans([max(cap, 128)] * (slots // max(cap, 128)))
    shifts = [0] + [(k + 1) // 2 if k % 2 else groups - k // 2 for k in range(1, groups)]

    def shift(array, distance):
        step = distance * GROUP
        return lax.ppermute(array, "blk", [(i, (i + step) % devices) for i in range(devices)])

    def swap(array, mask):
        return lax.ppermute(array, "blk", [(i, i ^ mask) for i in range(devices)])

    def exchange(array, start, axis, sign):
        size, out = array.shape[axis], []
        for k in range(start // cap, (start + size - 1) // cap + 1):
            a, b = max(k * cap - start, 0), min((k + 1) * cap - start, size)
            part = lax.slice_in_dim(array, a, b, axis=axis)
            out.append(shift(part, sign * shifts[k]) if shifts[k] else part)
        return join(out, axis)

    *blocks, slot = pack(groups, cap, units, embedding, row_owner, cluster_id)

    def tie(*arrays):
        return lax.optimization_barrier(arrays)

    def send(u):
        (start, size), out = units[u], []
        sub = min(cap, size)
        for i in range(size // sub):
            part = lax.slice_in_dim(blocks[u], i * (sub + PAD), (i + 1) * (sub + PAD))
            distance = shifts[(start + i * sub) // cap]
            out.append(shift(part, distance) if distance else part)
        return join(out, 0)

    def cross(parts):
        return [swap(part, 2) for part in parts]

    def core(parts):
        return [swap(part, 1) for part in parts]

    arrays = [[None] * BLOCKS for _ in range(4)]
    own, across, beside, beyond = arrays
    sent = [blocks[0], send(1)]
    heads = blocks[2], blocks[3]
    *heads, sent[1] = tie(*heads, sent[1])
    last = [blocks[3]]
    blocks[2:] = heads
    sent += [send(2), send(3)]
    own[:] = [sent[0]], [sent[1]], [sent[2]], sent[3:]
    every, row = (0, 1, 2, 3), [(0, slots)]
    floor = jnp.full((1, slots), -1.0, jnp.float32)

    def given(peers, blocks):
        return {(peer, k): arrays[peer][k] for peer in peers for k in blocks}

    if cap == slots // BLOCKS:
        opposite = cross(last)
        diagonal = core(opposite)
        across[0] = cross(own[0])
        own[0], own[1] = tie(own[0], own[1])
        beside[0] = core(own[0])
        for u in (1, 2):
            beside[u], across[u] = core(own[u]), cross(own[u])
        for u in range(3):
            beyond[u] = core(across[u])
        beside[3] = core(own[3])
        some = {(0, k): across[k] for k in range(3)}
        some |= {(0, 3): own[3], (1, 3): own[3], (2, 3): beside[3]}
        (theirs,) = compare(cap, row, [(0, 3, 3, (1, 2))], some, floor)
        mine = swap(theirs, 2)
        some = given(every, range(3)) | {(0, 3): own[0]}
        (best,) = compare(cap, row, [(0, 3, k, every) for k in range(3)], some, floor)
        jobs = [(3, 4, k, every) for k in range(3)] + [(0, 4, 3, (0, 2))]
        some = given(every, range(3)) | given((0, 2), (3,))
        best = list(compare(cap, pieces, jobs, some, best))
        for k in range(3):
            best[k] = jnp.maximum(best[k], mine[:, k * cap : (k + 1) * cap])
        backs = [exchange(b, low, 1, -1) for b, (low, _) in zip(best, pieces)]
        floor, best[0] = tie(floor, best[0])
        backs[0] = best[0]
        some = {(0, k): last for k in range(BLOCKS)} | {(1, 3): opposite, (3, 3): diagonal}
        (source,) = compare(cap, row, [(0, 1, 3, (1, 3))], some, floor)
        backs[3] = jnp.maximum(backs[3], source[:, :cap])
        return unpack(slot, backs).reshape(rows)

    for u in range(BLOCKS):
        beside[u], across[u] = core(own[u]), cross(own[u])
    for u in range(BLOCKS - 1):
        beyond[u] = core(across[u])

    best = floor
    jobs = [(0, 4, 0, every), (0, 4, 1, every), (0, 4, 2, every), (0, 4, 3, (0, 2))]
    some = given((0, 2), range(4)) | given((1, 3), range(3))
    (best,) = compare(cap, row, jobs, some, best)
    across[3][-1], best = tie(across[3][-1], best)
    beyond[3] = core(across[3])
    some = given((0,), range(4)) | given((1, 3), (3,))
    best = compare(cap, pieces, [(0, 4, 3, (1, 3))], some, best)
    backs = [exchange(b, low, 1, -1) for b, (low, _) in zip(best, pieces)]
    return unpack(slot, backs).reshape(rows)


def solution(mesh):
    placed = (P(("parts", "blk"), None), P(("parts", "blk")), P(("parts", "blk")))
    return jax.shard_map(
        on_device, mesh=mesh, in_specs=placed, out_specs=P(("parts", "blk")), check_vma=False
    )
```

```python
import jax
import jax.numpy as jnp
from jax import lax
from jax.experimental import pallas as pl
from jax.experimental.pallas import tpu as pltpu
from jax.sharding import PartitionSpec as P

GROUP = 4
BLOCKS = 4
UNITS = (4, 4, 4, 4)
PAD = 16
STEP = 512
GRANT = 16 << 20
NT = (((1,), (1,)), ((), ()))


def iota(shape, axis):
    return lax.broadcasted_iota(jnp.int32, shape, axis)


def spans(widths):
    start, out = 0, []
    for width in widths:
        out.append((start, width))
        start += width
    return out


def pack_kernel(groups, cap, units, emb_hbm, owner_hbm, cluster_hbm, *refs):
    blocks, refs = refs[: len(units)], refs[len(units) :]
    slot_ref, emb_ref, unit_ref, owner_ref, cluster_ref, sems = refs
    rows = emb_ref.shape[0]
    part = rows // 4
    copies = [
        pltpu.make_async_copy(owner_hbm, owner_ref, sems.at[0]),
        pltpu.make_async_copy(cluster_hbm, cluster_ref, sems.at[1]),
    ]
    for i in range(4):
        span = pl.ds(i * part, part)
        copies.append(pltpu.make_async_copy(emb_hbm.at[span], emb_ref.at[span], sems.at[2 + i]))
    for copy in copies:
        copy.start()
    earlier = (iota((rows, rows), 0) < iota((rows, rows), 1)).astype(jnp.bfloat16)
    mine = lax.axis_index("blk") // GROUP
    copies[0].wait()
    rel = ((owner_ref[...] >> 2) - mine + groups) & (groups - 1)
    place = jnp.where(rel > groups // 2, 2 * (groups - rel), jnp.maximum(2 * rel - 1, 0))
    member = iota((max(groups, 16), rows), 0) == place
    count = jnp.dot(member.astype(jnp.bfloat16), earlier, preferred_element_type=jnp.float32)
    rank = jnp.sum(jnp.where(member, count, 0.0), axis=0, keepdims=True)
    slot = place * cap + rank.astype(jnp.int32)
    slot_ref[...] = slot
    copies[1].wait()
    label = ((cluster_ref[...] & 15) + 1).astype(jnp.float32).astype(jnp.bfloat16)
    label = jnp.broadcast_to(label, (PAD, rows))
    for i in range(4):
        copies[2 + i].wait()
        x = emb_ref[i * part : (i + 1) * part, :]
        squares = jnp.sum(x * x, axis=1, keepdims=True)
        unit_ref[i * part : (i + 1) * part, :] = (x * lax.rsqrt(squares + 1e-06)).astype(
            jnp.bfloat16
        )
    unit = unit_ref[...]
    for ref, (start, size) in zip(blocks, units):
        hot = (iota((size, rows), 0) + start == slot).astype(jnp.bfloat16)
        packed = jnp.dot(hot, unit, preferred_element_type=jnp.float32).astype(jnp.bfloat16)
        marks = lax.dot_general(label, hot, NT, preferred_element_type=jnp.float32)
        marks = (marks - 1.0).astype(jnp.bfloat16)
        sub = min(cap, size)
        for i in range(size // sub):
            low = i * (sub + PAD)
            ref[low : low + sub, :] = packed[i * sub : (i + 1) * sub, :]
            ref[low + sub : low + sub + PAD, :] = jnp.zeros((PAD, unit.shape[1]), jnp.bfloat16)
            ref[low + sub : low + sub + PAD, 0:sub] = marks[:, i * sub : (i + 1) * sub]


def pack(groups, cap, units, embedding, owner, cluster):
    rows, width = embedding.shape
    return pl.pallas_call(
        lambda *refs: pack_kernel(groups, cap, units, *refs),
        in_specs=[pl.BlockSpec(memory_space=pltpu.HBM)] * 3,
        out_shape=[
            jax.ShapeDtypeStruct((n + n // min(cap, n) * PAD, width), jnp.bfloat16)
            for _, n in units
        ]
        + [jax.ShapeDtypeStruct((1, rows), jnp.int32)],
        scratch_shapes=[
            pltpu.VMEM((rows, width), jnp.float32),
            pltpu.VMEM((rows, width), jnp.bfloat16),
            pltpu.VMEM((1, rows), jnp.int32),
            pltpu.VMEM((1, rows), jnp.int32),
            pltpu.SemaphoreType.DMA((6,)),
        ],
        name="pack",
    )(embedding, owner.reshape(1, rows), cluster.reshape(1, rows))


def compare_kernel(cap, outs, jobs, names, *refs):
    best_ref, refs = refs[0], refs[1:]
    given = {}
    for name, ref in zip(names, refs):
        given.setdefault(name, []).append(ref)
    refs = refs[len(names) :]
    outputs, scratch = refs[: len(outs)], list(refs[len(outs) :])
    query_ref = scratch.pop()
    size = query_ref.shape[0] // BLOCKS

    def unfold(parts, target, low):
        for ref in parts:
            sub = min(cap, size // len(parts))
            for start in range(0, ref.shape[0], sub + PAD):
                target[low : low + sub, :] = ref[start : start + sub, :]
                low += sub

    keys, marks = {}, {}
    for (peer, k), parts in given.items():
        sub = min(cap, size // len(parts))
        row = [
            ref[start + sub : start + sub + PAD, 0:sub].astype(jnp.float32)
            for ref in parts
            for start in range(0, ref.shape[0], sub + PAD)
        ]
        marks[peer, k] = jnp.concatenate(row, axis=1)[0:1, :]
        if peer == 0:
            unfold(parts, query_ref, k * size)
            keys[peer, k] = query_ref.at[k * size : (k + 1) * size]
        elif size == sub:
            keys[peer, k] = parts[0].at[0:size]
        else:
            keys[peer, k] = scratch.pop()
            unfold(parts, keys[peer, k], 0)
    columns = {}
    for k in range(BLOCKS):
        table = [marks.get((peer, k), marks[0, k]) for peer in range(4)]
        columns[k] = jnp.concatenate(table * 2, axis=0).T
    near = jnp.concatenate([marks[0, k] for k in range(BLOCKS)], axis=1)
    bests = [best_ref[:, k * size : (k + 1) * size] for k in range(BLOCKS)]
    for low, high, k, peers in jobs:
        for left in range(low, high, STEP // size):
            right = min(left + STEP // size, high)
            span = slice(left * size, right * size)
            row = near[0:1, span]
            best = None
            for peer in peers:
                scores = lax.dot_general(
                    keys[peer, k][...],
                    query_ref[span, :],
                    NT,
                    preferred_element_type=jnp.float32,
                )
                allowed = columns[k][:, peer : peer + 1] == row
                if peer == 0 and left <= k < right:
                    shift = (k - left) * size
                    allowed = allowed & (iota(scores.shape, 0) + shift != iota(scores.shape, 1))
                top = jnp.max(jnp.where(allowed, scores, -1.0), axis=0, keepdims=True)
                best = top if best is None else jnp.maximum(best, top)
            for q in range(left, right):
                part = best[:, (q - left) * size : (q - left + 1) * size]
                bests[q] = jnp.maximum(bests[q], part)
    for q in range(BLOCKS):
        spread(outputs, outs, q * size, bests[q])


def spread(refs, outs, start, row):
    for ref, (low, width) in zip(refs, outs):
        a, b = max(low, start), min(low + width, start + row.shape[1])
        if a < b:
            ref[:, a - low : b - low] = row[:, a - start : b - start]


def compare(cap, outs, jobs, blocks, best):
    slots, width = best.shape[1], blocks[0, 0][0].shape[1]
    size = slots // BLOCKS
    tiles = sum((high - low) * len(peers) for low, high, _, peers in jobs)
    folded = [key for key, parts in blocks.items() if key[0] and size > min(cap, size // len(parts))]
    names = tuple(key for key, parts in blocks.items() for _ in parts)
    return pl.pallas_call(
        lambda *refs: compare_kernel(cap, outs, jobs, names, *refs),
        out_shape=[jax.ShapeDtypeStruct((1, n), jnp.float32) for _, n in outs],
        scratch_shapes=[pltpu.VMEM((size, width), jnp.bfloat16)] * len(folded)
        + [pltpu.VMEM((slots, width), jnp.bfloat16)],
        compiler_params=pltpu.CompilerParams(vmem_limit_bytes=GRANT),
        cost_estimate=pl.CostEstimate(
            flops=2 * tiles * size * size * width, bytes_accessed=0, transcendentals=0
        ),
        name=f"compare{len(jobs)}_{tiles}",
    )(best, *[part for parts in blocks.values() for part in parts])


def unpack_kernel(slot_ref, *refs):
    out_ref = refs[-1]
    slot = slot_ref[...]
    rows = slot.shape[1]
    total = jnp.zeros((8, rows), jnp.float32)
    start = 0
    for ref in refs[:-1]:
        size = ref.shape[1]
        column = jnp.broadcast_to(ref[...], (8, size)).T[:, 0:1]
        hit = iota((size, rows), 0) + start == slot
        part = jnp.where(hit, column, 0.0)
        total = total + jnp.sum(part.reshape(size // 8, 8, rows), axis=0)
        start += size
    out_ref[...] = jnp.sum(total, axis=0, keepdims=True)


def unpack(slot, backs):
    return pl.pallas_call(
        unpack_kernel,
        out_shape=jax.ShapeDtypeStruct(slot.shape, jnp.float32),
        compiler_params=pltpu.CompilerParams(vmem_limit_bytes=GRANT),
        name="unpack",
    )(slot, *backs)


def join(parts, axis):
    return parts[0] if len(parts) == 1 else jnp.concatenate(parts, axis=axis)


def on_device(embedding, row_owner, cluster_id):
    rows, _ = embedding.shape
    devices = lax.axis_size("blk")
    groups = devices // GROUP
    cap = GROUP * max(2, 2 * rows // devices)
    slots = groups * cap
    units = spans([slots // 16 * n for n in UNITS])
    pieces = spans([max(cap, 128)] * (slots // max(cap, 128)))
    shifts = [0] + [(k + 1) // 2 if k % 2 else groups - k // 2 for k in range(1, groups)]

    def shift(array, distance):
        step = distance * GROUP
        return lax.ppermute(array, "blk", [(i, (i + step) % devices) for i in range(devices)])

    def swap(array, mask):
        return lax.ppermute(array, "blk", [(i, i ^ mask) for i in range(devices)])

    def exchange(array, start, axis, sign):
        size, out = array.shape[axis], []
        for k in range(start // cap, (start + size - 1) // cap + 1):
            a, b = max(k * cap - start, 0), min((k + 1) * cap - start, size)
            part = lax.slice_in_dim(array, a, b, axis=axis)
            out.append(shift(part, sign * shifts[k]) if shifts[k] else part)
        return join(out, axis)

    *blocks, slot = pack(groups, cap, units, embedding, row_owner, cluster_id)

    def tie(*arrays):
        return lax.optimization_barrier(arrays)

    def send(u):
        (start, size), out = units[u], []
        sub = min(cap, size)
        for i in range(size // sub):
            part = lax.slice_in_dim(blocks[u], i * (sub + PAD), (i + 1) * (sub + PAD))
            distance = shifts[(start + i * sub) // cap]
            out.append(shift(part, distance) if distance else part)
        return join(out, 0)

    def cross(parts):
        return [swap(part, 2) for part in parts]

    def core(parts):
        return [swap(part, 1) for part in parts]

    arrays = [[None] * BLOCKS for _ in range(4)]
    own, across, beside, beyond = arrays
    sent = [blocks[0], send(1)]
    heads = blocks[2], blocks[3]
    *heads, sent[1] = tie(*heads, sent[1])
    last = [blocks[3]]
    blocks[2:] = heads
    sent += [send(2), send(3)]
    own[:] = [sent[0]], [sent[1]], [sent[2]], sent[3:]
    every, row = (0, 1, 2, 3), [(0, slots)]
    floor = jnp.full((1, slots), -1.0, jnp.float32)

    def given(peers, blocks):
        return {(peer, k): arrays[peer][k] for peer in peers for k in blocks}

    if cap == slots // BLOCKS:
        opposite = cross(last)
        diagonal = core(opposite)
        across[0] = cross(own[0])
        own[0], own[1] = tie(own[0], own[1])
        beside[0] = core(own[0])
        for u in (1, 2):
            beside[u], across[u] = core(own[u]), cross(own[u])
        for u in range(3):
            beyond[u] = core(across[u])
        beside[3] = core(own[3])
        some = {(0, k): across[k] for k in range(3)}
        some |= {(0, 3): own[3], (1, 3): own[3], (2, 3): beside[3]}
        (theirs,) = compare(cap, row, [(0, 3, 3, (1, 2))], some, floor)
        mine = swap(theirs, 2)
        jobs = [(0, 4, k, every) for k in range(3)] + [(0, 4, 3, (0, 2))]
        some = given(every, range(3)) | given((0, 2), (3,))
        best = list(compare(cap, pieces, jobs, some, floor))
        for k in range(3):
            best[k] = jnp.maximum(best[k], mine[:, k * cap : (k + 1) * cap])
        backs = [exchange(b, low, 1, -1) for b, (low, _) in zip(best, pieces)]
        floor, best[0] = tie(floor, best[0])
        backs[0] = best[0]
        some = {(0, k): last for k in range(BLOCKS)} | {(1, 3): opposite, (3, 3): diagonal}
        (source,) = compare(cap, row, [(0, 1, 3, (1, 3))], some, floor)
        backs[3] = jnp.maximum(backs[3], source[:, :cap])
        return unpack(slot, backs).reshape(rows)

    for u in range(BLOCKS):
        beside[u], across[u] = core(own[u]), cross(own[u])
    for u in range(BLOCKS - 1):
        beyond[u] = core(across[u])

    best = floor
    jobs = [(0, 4, 0, every), (0, 4, 1, every), (0, 4, 2, every), (0, 4, 3, (0, 2))]
    some = given((0, 2), range(4)) | given((1, 3), range(3))
    (best,) = compare(cap, row, jobs, some, best)
    across[3][-1], best = tie(across[3][-1], best)
    beyond[3] = core(across[3])
    some = given((0,), range(4)) | given((1, 3), (3,))
    best = compare(cap, pieces, [(0, 4, 3, (1, 3))], some, best)
    backs = [exchange(b, low, 1, -1) for b, (low, _) in zip(best, pieces)]
    return unpack(slot, backs).reshape(rows)


def solution(mesh):
    placed = (P(("parts", "blk"), None), P(("parts", "blk")), P(("parts", "blk")))
    return jax.shard_map(
        on_device, mesh=mesh, in_specs=placed, out_specs=P(("parts", "blk")), check_vma=False
    )
```
